256 devices in a mesh: row: 64 (over z, x, core), ba: 4 (over y).
Axes of the slice: x: 4, y: 4, z: 8, core: 2. Of those that a mesh axis runs over, the one named last changes fastest.
Arguments:
- constants: float32 [64, 192, 36864], P('row', 'ba'), may hold values from -6 to 6
- current_modes: float32 [64, 2, 192, 4], P('row', None, 'ba'), may hold values from -0.4375 to 0.4375
- owner_id: int32 [1], replicated, may hold values from 0 to 63
- live_count: int32 [64], P('row'), may hold values from 0 to 1, as said below
- triplets: int32 [64, 6], P('row'), may hold values from -3 to 3
- center_point: int32 [3], replicated, may hold values from 0 to 31
- pair_points: int32 [512, 3], P('row'), may hold values from 0 to 31
- first_vectors: float32 [512, 2, 36864], P('row'), may hold values from -0.4375 to 0.4375
- second_vectors: float32 [512, 2, 36864], P('row'), may hold values from -0.4375 to 0.4375
Outputs:
- strength: float32 [512, 4, 36864], P('row', 'ba')
The draws below stay inside these ranges and needn't reach their ends.
Inputs may be any that keep to these rules, and one draw needn't show every extreme that they name: Shard j uses its first live_count[j] slots; the constants and triplets of the other slots are ignored. A shard may use none. Some shard uses all 1 slots.
All inputs are finite; a program needn't handle non-finite values.
Results may differ from the reference program's by a relative error of at most 0.00008.
Values sent between devices are 32-bit elements; how exact they have to be, the bound alone decides.
A program may use at most 128 MiB of HBM per device.

```python
import math
import jax
import jax.numpy as jnp
from jax import lax

B = 192
BB = 36864
G = 32
R_SLOT = 1
SHARDS = 64
R = 64
QP = 512
NB = 4


def draw_live_count(key, part):
    key_pick = jax.random.fold_in(key, 11)
    key_spread = jax.random.fold_in(key, 12)
    key_full = jax.random.fold_in(key, 13)
    picked = jax.random.randint(key_pick, (SHARDS,), 0, 5)
    spread = jax.random.randint(key_spread, (SHARDS,), 0, R_SLOT + 1)
    counts = jnp.where(picked < 2, 0, spread)
    full_shard = jax.random.randint(key_full, (), 0, SHARDS)
    counts = jnp.where(jnp.arange(SHARDS) == full_shard, R_SLOT, counts)
    return counts.astype(jnp.int32)


def with_ends(values, own_key, low, top_value):
    longest = values.shape.index(max(values.shape))
    spots = []
    for shift in (0, 1):
        where = [jax.random.randint(jax.random.fold_in(own_key, axis), (), 0, length) for axis, length in enumerate(values.shape)]
        where[longest] = (where[longest] + shift) % values.shape[longest]
        spots.append(tuple(where))
    return values.at[spots[0]].set(low).at[spots[1]].set(top_value)


def block_levels(rng, dims, pieces, least, high):
    def one(axis_at, shards_of):
        steps = jax.random.uniform(jax.random.fold_in(jax.random.fold_in(rng, 6), axis_at), (shards_of,), jnp.float32, least / len(pieces), high / len(pieces))
        return jnp.repeat(jnp.exp(steps), dims[axis_at] // shards_of).reshape((-1,) + (1,) * (len(dims) - axis_at - 1))

    level = one(*pieces[0])
    for cut in pieces[1:]:
        level = level * one(*cut)
    return level


def normal_values(own_key, extent, width, most, cuts=(), held_as=jnp.bfloat16):
    values = width * jax.random.normal(own_key, extent, jnp.float32)
    if cuts:
        values = values * block_levels(own_key, extent, cuts, -0.22, 0.18)
    return jnp.clip(values, -most, most).astype(held_as)


def setup_inputs(seed: int = 0) -> dict:
    key_of = jax.random.split(jax.random.key(seed), 10)
    return {
        "constants": normal_values(key_of[0], (R, B, BB), 1.0, 6.0, ((0, 64), (1, 4)), jnp.float32),
        "current_modes": normal_values(key_of[1], (SHARDS, 2, B, NB), B ** -0.5, 0.4375, ((0, 64), (2, 4)), jnp.float32),
        "owner_id": jax.random.randint(key_of[2], (1,), 0, SHARDS).astype(jnp.int32),
        "live_count": draw_live_count(jax.random.fold_in(key_of[9], 71), 0),
        "triplets": with_ends(jax.random.randint(key_of[4], (R, 6), -3, 4), jax.random.fold_in(key_of[4], 1), -3, 3).astype(jnp.int32),
        "center_point": jax.random.randint(key_of[5], (3,), 0, G).astype(jnp.int32),
        "pair_points": with_ends(jax.random.randint(key_of[6], (QP, 3), 0, G), jax.random.fold_in(key_of[6], 1), 0, G - 1).astype(jnp.int32),
        "first_vectors": normal_values(key_of[7], (QP, 2, BB), B ** -0.5, 0.4375, ((0, 64),), jnp.float32),
        "second_vectors": normal_values(key_of[8], (QP, 2, BB), B ** -0.5, 0.4375, ((0, 64),), jnp.float32),
    }


HIGHEST = lax.Precision.HIGHEST
FULL_TURN = 2.0 * math.pi


def rotation_table(pair_rows, shift_rows, grid_size):
    turns = jnp.sum(pair_rows[:, :, None] * shift_rows[None, 0:3, :], axis=1) - shift_rows[3][None, :]
    angle = jnp.mod(turns, grid_size).astype(jnp.float32) * (FULL_TURN / grid_size)
    cosine = jnp.cos(angle)
    sine = jnp.sin(angle)
    upper_row = jnp.stack([cosine, -sine], axis=1)
    lower_row = jnp.stack([sine, cosine], axis=1)
    return jnp.stack([upper_row, lower_row], axis=1)


def complex_block(vectors, branches):
    pair_count = vectors.shape[0]
    real_part = vectors[:, 0].reshape(pair_count, branches, branches)
    imag_part = vectors[:, 1].reshape(pair_count, branches, branches)
    upper_row = jnp.stack([real_part, -imag_part], axis=1)
    lower_row = jnp.stack([imag_part, real_part], axis=1)
    return jnp.stack([upper_row, lower_row], axis=1)


def strengths(phase_sum, first_vectors, second_vectors, branches, total_slots):
    pair_count = phase_sum.shape[0]
    band_count = phase_sum.shape[1]
    shaped = phase_sum.reshape(pair_count, band_count, 2, branches, branches)
    partial_sum = jnp.einsum("knibc,koicm->knobm", shaped, complex_block(second_vectors, branches), precision=HIGHEST)
    amplitude = jnp.einsum("kojbp,knjbm->knopm", complex_block(first_vectors, branches), partial_sum, precision=HIGHEST)
    result = (amplitude[:, :, 0] * amplitude[:, :, 0] + amplitude[:, :, 1] * amplitude[:, :, 1]) / total_slots
    return result.reshape(pair_count, band_count, branches * branches)


def reference(constants, current_modes, owner_id, live_count, triplets, center_point, pair_points, first_vectors, second_vectors):
    eigen = current_modes[owner_id[0]]
    slot_index = jnp.arange(R, dtype=jnp.int32)
    weight = ((slot_index % R_SLOT) < live_count[slot_index // R_SLOT]).astype(jnp.float32)
    contracted = jnp.einsum("san,rax->nsrx", eigen, constants, precision=HIGHEST)
    contracted = contracted * weight[None, None, :, None]
    second_cell = triplets[:, 3:6]
    offsets = triplets[:, 0:3] - second_cell
    point_shift = jnp.sum(second_cell * center_point[None, :], axis=1)
    shift_rows = jnp.concatenate([offsets.T, point_shift[None, :]], axis=0)
    rotation = rotation_table(pair_points, shift_rows, G)
    phase_sum = jnp.einsum("kuir,nirx->knux", rotation, contracted, precision=HIGHEST)
    return strengths(phase_sum, first_vectors, second_vectors, B, R)
```

```python
import functools
import math

import jax
import jax.numpy as jnp
from jax import lax
from jax.experimental import pallas as pl
from jax.experimental.pallas import tpu as pltpu
from jax.sharding import PartitionSpec as P

B = 192
G = 32
Z, X = 8, 4
Q = 2 * X
R = Z * Q
LANES = 128
TILES = B * B // LANES
SHARE = TILES // Q
J = 3
TT = SHARE // J
BLK = 2 * TT
HALF = Q // 2
PAIRS = 8
KO = 2 * PAIRS
MESH = pl.DeviceIdType.MESH
F32 = jnp.float32
BF16 = jnp.bfloat16


def split(value):
    high = value.astype(BF16)
    return high, (value - high.astype(F32)).astype(BF16)


def dot(a, b):
    return lax.dot_general(a, b, (((1,), (0,)), ((), ())), preferred_element_type=F32)


def dot3(ah, al, bh, bl):
    return dot(ah, bh) + dot(al, bh) + dot(ah, bl)


def kernel(
    sum_ref, points_ref, live_ref, const_ref, first_ref, second_ref, out_ref,
    const_v, first_v, second_v, got1, got2, rot, lhs, term, part1, part2, final,
    gathered, phase_out, phase_in, square, first_t, second_m,
    const_sem, vec_sem, s1, r1, s2, r2, sy1, ry1, sy2, ry2, sc, rc, sz, rz, sp, rp,
):
    row = lax.axis_index("row")
    y = lax.axis_index("ba")
    z = row // Q
    q = row % Q
    x = q // 2
    core = q % 2
    ya = y + 1 - 2 * (y % 2)
    yb = 3 - y
    y2 = (y + 2) % 4

    def qpeer(i):
        return ((x + i // 2) % X) * 2 + (core + i % 2) % 2

    def zpeer(i):
        return (z + i) % Z

    const_copies = {}
    for j in range(J):
        for p in range(Q):
            copy = pltpu.make_async_copy(
                const_ref.at[:, pl.ds((p * SHARE + j * TT) * LANES, TT * LANES)],
                const_v.at[j, p],
                const_sem.at[j, p],
            )
            copy.start()
            const_copies[j, p] = copy
    second_copy = pltpu.make_async_copy(second_ref, second_v, vec_sem.at[0])
    second_copy.start()
    first_copy = pltpu.make_async_copy(first_ref, first_v, vec_sem.at[1])
    first_copy.start()

    barrier = pltpu.get_barrier_semaphore()
    for i in range(1, Z):
        pl.semaphore_signal(barrier, inc=1, device_id=(zpeer(i) * Q + q, y), device_id_type=MESH)
    for i in range(1, Q):
        pl.semaphore_signal(barrier, inc=1, device_id=(z * Q + qpeer(i), y), device_id_type=MESH)
    for other in (ya, yb):
        pl.semaphore_signal(barrier, inc=1, device_id=(row, other), device_id_type=MESH)
    pl.semaphore_wait(barrier, Z - 1 + Q - 1 + 2)

    def remote(src, dst, send, recv, device):
        return pltpu.make_async_remote_copy(
            src_ref=src, dst_ref=dst, send_sem=send, recv_sem=recv,
            device_id=device, device_id_type=MESH,
        )

    copies1 = []
    for i in range(1, Z):
        copy = remote(sum_ref, got1.at[i], s1.at[i], r1.at[i], (zpeer(i) * Q + q, y))
        copy.start()
        copies1.append(copy)
    for copy in copies1:
        copy.wait_recv()
    total = sum_ref[...]
    for i in range(1, Z):
        total = total + got1[i]
    got2[q, 0:16] = total
    got2[q, 16:32] = points_ref[...]
    copies2 = []
    for i in range(1, Q):
        copy = remote(got2.at[q], got2.at[q], s2.at[i], r2.at[i], (z * Q + qpeer(i), y))
        copy.start()
        copies2.append(copy)

    def paired(ref, k, start, stride):
        tiles = [ref[k, pl.ds(start + stride // 3 * i, B // 2, stride=stride), :] for i in range(3)]
        even = jnp.concatenate(tiles[0:2], axis=1)
        odd = pltpu.roll(jnp.concatenate(tiles[1:3], axis=1), 192, 1)
        return even, odd

    def prepare_second(k, carry):
        for o in range(2):
            even, odd = paired(second_v, k, o, 6)
            for i in range(2):
                lanes = slice(i * LANES, (i + 1) * LANES)
                square[i, pl.ds(0, B // 2, stride=2), :] = even[:, lanes]
                square[i, pl.ds(1, B // 2, stride=2), :] = odd[:, lanes]
            high, low = split(jnp.concatenate([square[0, 0:B, :], square[1, 0:B, :]], axis=1))
            zero = jnp.zeros((256 - B, 256), BF16)
            second_m[k, o, 0] = jnp.concatenate([high, zero], axis=0)
            second_m[k, o, 1] = jnp.concatenate([low, zero], axis=0)
        return carry

    def prepare_first(k, carry):
        for o in range(2):
            even, odd = paired(first_v, k, o, 6)
            zero = jnp.zeros((256 - B, 256), F32)
            turned = jnp.transpose(jnp.concatenate([even, odd, zero], axis=0))
            for i in range(2):
                lanes = slice(i * LANES, (i + 1) * LANES)
                square[i] = turned[:, lanes]
                for parity in range(2):
                    high, low = split(square[i, pl.ds(parity, B // 2, stride=2), :])
                    rows = slice(parity * (B // 2), (parity + 1) * (B // 2))
                    first_t[k, o, 0, rows, lanes] = high
                    first_t[k, o, 1, rows, lanes] = low
        return carry

    second_copy.wait()
    lax.fori_loop(0, PAIRS, prepare_second, 0)

    for copy in copies2:
        copy.wait_recv()
    total = got2[0, 0:16]
    for i in range(1, Q):
        total = total + got2[i, 0:16]
    points = jnp.concatenate([got2[i, 16:32] for i in range(Q)], axis=0)
    turns = -total[11:12]
    for axis in range(3):
        turns = turns + points[:, axis : axis + 1] * total[8 + axis : 9 + axis]
    lane = lax.broadcasted_iota(jnp.int32, (Q * KO, LANES), 1)
    line = lax.broadcasted_iota(jnp.int32, (Q * KO, LANES), 0)
    turns = turns + jnp.where(lane >= R, 8.0, 0.0) - jnp.where(line % 2 == 1, 8.0, 0.0)
    turns = turns - G * jnp.floor(turns * (1.0 / G))
    high, low = split(jnp.cos(turns * (2.0 * math.pi / G)))
    rot[:, 0:128] = high
    rot[:, 128:256] = low
    eigen = total[0:8] * jnp.where(live_ref[0] > 0, 1.0, 0.0)
    high, low = split(eigen)
    lane8 = lax.broadcasted_iota(jnp.int32, (8, LANES), 1)
    lhs[...] = jnp.concatenate(
        [high.astype(F32), jnp.where(lane8 < 48, low.astype(F32), 0.0)], axis=0
    ).astype(BF16)

    def contract(j):
        def step(p, carry):
            pltpu.make_async_copy(const_ref.at[:, pl.ds(0, TT * LANES)], const_v.at[j, p], const_sem.at[j, p]).wait()
            high, low = split(const_v[j, p])
            both = dot(lhs[:, 0:96], jnp.concatenate([high, low], axis=0))
            both = both[0:8] + both[8:16]
            for t in range(TT):
                term[j, p, pl.ds(t, 8, stride=TT), :] = both[:, t * LANES : (t + 1) * LANES]
            return carry

        lax.fori_loop(0, Q, step, 0)

    waits = []

    def go(copy):
        copy.start()
        waits.append(copy)
        return copy

    def band(j, h, n):
        return term.at[j, pl.ds(HALF * h, HALF), pl.ds(pl.multiple_of(n * BLK, 8), BLK), :]

    y1, yy2, c2a, ring, p2a = {}, {}, {}, {}, {}

    def y1_start(j):
        for h, other in enumerate((ya, yb)):
            for slot, n in enumerate((other, y2)):
                y1[j, h, slot] = go(remote(
                    band(j, h, n), part1.at[j, h, slot], sy1.at[j, h, slot], ry1.at[j, h, slot], (row, other)
                ))

    def y2_start(j):
        for h, other in enumerate((yb, ya)):
            y1[j, h, 1].wait_recv()
            mine = band(j, h, other)
            mine[...] = mine[...] + part1[j, h, 1]
            yy2[j, h] = go(remote(mine, part2.at[j, h], sy2.at[j, h], ry2.at[j, h], (row, other)))

    def slot_rows(r, count=1):
        return pl.ds(pl.multiple_of(r * BLK, 8), count * BLK)

    def c2a_start(j):
        for h in range(2):
            y1[j, h, 0].wait_recv()
            yy2[j, h].wait_recv()
            final[j, HALF * h : HALF * (h + 1)] = band(j, h, y)[...] + part1[j, h, 0] + part2[j, h]
        gathered[j, slot_rows(row), :] = final[j, q]
        for i in range(1, Q):
            c2a[j, i] = go(remote(
                final.at[j, qpeer(i)], gathered.at[j, slot_rows(row), :], sc.at[j, i], rc.at[j, i],
                (z * Q + qpeer(i), y),
            ))

    def ring_start(j, i):
        if i == 1:
            for n in range(1, Q):
                c2a[j, n].wait_recv()
        else:
            for side in range(2):
                ring[j, i - 1, side].wait_recv()
        for side, sign in enumerate((1, -1)):
            base = ((z + Z - sign * (i - 1)) % Z) * Q
            rows = slot_rows(base, Q) if i < 4 else slot_rows(base + HALF * side, HALF)
            block = gathered.at[j, rows, :]
            ring[j, i, side] = go(remote(
                block, block, sz.at[j, i, side], rz.at[j, i, side], (((z + Z + sign) % Z) * Q + q, y)
            ))

    def phase(j):
        for side in range(2):
            ring[j, 4, side].wait_recv()

        def step(u, carry):
            cols = []
            for v in range(2):
                t = 2 * u + v
                cols.append(jnp.concatenate(
                    [gathered[j, pl.ds(s * TT + t, R, stride=BLK), :] for s in range(2)], axis=0
                ))
            high, low = split(jnp.concatenate(cols, axis=1))
            value = dot(rot[...], jnp.concatenate([high, high], axis=0)) + dot(rot[:, 0:128], low)
            for v in range(2):
                for d in range(Q):
                    phase_out[j, d, pl.ds(pl.multiple_of((2 * u + v) * KO, 8), KO), :] = value[
                        d * KO : (d + 1) * KO, v * LANES : (v + 1) * LANES
                    ]
            return carry

        lax.fori_loop(0, TT // 2, step, 0)
        rows = pl.ds(pl.multiple_of((q * SHARE + j * TT) * KO, 8), TT * KO)
        for i in range(1, Q):
            p2a[j, i] = go(remote(
                phase_out.at[j, qpeer(i)], phase_in.at[rows, :], sp.at[j, i], rp.at[j, i], (z * Q + qpeer(i), y)
            ))
        phase_in[rows, :] = phase_out[j, q]

    for j in range(J):
        contract(j)
        y1_start(j)
    for j in range(J):
        y2_start(j)
    for j in range(J):
        c2a_start(j)
    for j in range(J):
        ring_start(j, 1)
    first_copy.wait()
    lax.fori_loop(0, PAIRS, prepare_first, 0)
    for i in range(2, 5):
        for j in range(J):
            ring_start(j, i)
    for j in range(J):
        phase(j)
    for j in range(J):
        for i in range(1, Q):
            p2a[j, i].wait_recv()

    def finish(k, carry):
        planes = []
        for o in range(2):
            tiles = [
                phase_in[pl.ds(KO * i + 2 * k + o, B // 2, stride=3 * KO), :] for i in range(3)
            ]
            even = jnp.concatenate(tiles[0:2], axis=1)
            odd = pltpu.roll(jnp.concatenate(tiles[1:3], axis=1), 192, 1)
            planes.append(split(jnp.concatenate([even, odd], axis=0)))
        (prh, prl), (pih, pil) = planes
        wr = (second_m[k, 0, 0], second_m[k, 0, 1])
        wi = (second_m[k, 1, 0], second_m[k, 1, 1])
        real = dot3(prh, prl, *wr) - dot3(pih, pil, *wi)
        imag = dot3(prh, prl, *wi) + dot3(pih, pil, *wr)
        zero = jnp.zeros((256 - B, 256), F32)
        tr = split(jnp.concatenate([real, zero], axis=0))
        ti = split(jnp.concatenate([imag, zero], axis=0))
        vr = (first_t[k, 0, 0], first_t[k, 0, 1])
        vi = (first_t[k, 1, 0], first_t[k, 1, 1])
        real = dot3(*vr, *tr) - dot3(*vi, *ti)
        imag = dot3(*vr, *ti) + dot3(*vi, *tr)
        value = (real * real + imag * imag) * (1.0 / R)
        even = value[0 : B // 2]
        odd = pltpu.roll(value[B // 2 : B], 64, 1)
        lane = lax.broadcasted_iota(jnp.int32, (B // 2, LANES), 1)
        out_ref[k, pl.ds(0, B // 2, stride=3), :] = even[:, 0:LANES]
        out_ref[k, pl.ds(1, B // 2, stride=3), :] = jnp.where(
            lane < 64, even[:, LANES:], odd[:, 0:LANES]
        )
        out_ref[k, pl.ds(2, B // 2, stride=3), :] = odd[:, LANES:]
        return carry

    lax.fori_loop(0, PAIRS, finish, 0)
    for copy in copies1 + copies2 + waits:
        copy.wait_send()


def linear(vectors):
    tiles = vectors.reshape(PAIRS, 2, TILES, LANES)
    return tiles.transpose(0, 2, 1, 3).reshape(PAIRS, 2 * TILES, LANES)


def body(
    constants,
    current_modes,
    owner_id,
    live_count,
    triplets,
    center_point,
    pair_points,
    first_vectors,
    second_vectors,
):
    row = lax.axis_index("row")
    eigen = jnp.where(row == owner_id[0], current_modes[0], 0.0)
    eigen = eigen.transpose(2, 0, 1).reshape(8, 48)
    eigen = jnp.concatenate([eigen, eigen, jnp.zeros((8, LANES - 96), F32)], axis=1)
    second_cell = triplets[0, 3:6]
    offsets = triplets[0, 0:3] - second_cell
    shift = jnp.sum(second_cell * center_point)
    geometry = jnp.concatenate([offsets, shift[None], jnp.zeros((4,), jnp.int32)]).astype(F32)
    lane = jnp.arange(LANES, dtype=jnp.int32)
    geometry = jnp.where((lane % R == row)[None, :], geometry[:, None], 0.0)
    sums = jnp.concatenate([eigen, geometry], axis=0)
    points = jnp.pad(jnp.repeat(pair_points.astype(F32), 2, axis=0), ((0, 0), (0, LANES - 3)))

    vmem = pl.BlockSpec(memory_space=pltpu.VMEM)
    anywhere = pl.BlockSpec(memory_space=pl.ANY)
    dma = pltpu.SemaphoreType.DMA
    out = pl.pallas_call(
        kernel,
        out_shape=jax.ShapeDtypeStruct((PAIRS, TILES, LANES), F32),
        in_specs=[vmem, vmem, pl.BlockSpec(memory_space=pltpu.SMEM), anywhere, anywhere, anywhere],
        out_specs=vmem,
        scratch_shapes=[
            pltpu.VMEM((J, Q, 48, TT * LANES), F32),
            pltpu.VMEM((PAIRS, 2 * TILES, LANES), F32),
            pltpu.VMEM((PAIRS, 2 * TILES, LANES), F32),
            pltpu.VMEM((Z, 16, LANES), F32),
            pltpu.VMEM((Q, 32, LANES), F32),
            pltpu.VMEM((Q * KO, 256), BF16),
            pltpu.VMEM((16, LANES), BF16),
            pltpu.VMEM((J, Q, 4 * BLK, LANES), F32),
            pltpu.VMEM((J, 2, 2, HALF, BLK, LANES), F32),
            pltpu.VMEM((J, 2, HALF, BLK, LANES), F32),
            pltpu.VMEM((J, Q, BLK, LANES), F32),
            pltpu.VMEM((J, R * BLK, LANES), F32),
            pltpu.VMEM((J, Q, TT * KO, LANES), F32),
            pltpu.VMEM((TILES * KO, LANES), F32),
            pltpu.VMEM((2, 256, LANES), F32),
            pltpu.VMEM((PAIRS, 2, 2, B, 256), BF16),
            pltpu.VMEM((PAIRS, 2, 2, 256, 256), BF16),
            dma((J, Q)), dma((2,)),
            dma((Z,)), dma((Z,)), dma((Q,)), dma((Q,)),
            dma((J, 2, 2)), dma((J, 2, 2)), dma((J, 2)), dma((J, 2)),
            dma((J, Q)), dma((J, Q)), dma((J, 5, 2)), dma((J, 5, 2)), dma((J, Q)), dma((J, Q)),
        ],
        compiler_params=pltpu.CompilerParams(
            collective_id=0, has_side_effects=True, vmem_limit_bytes=56 * 2**20
        ),
    )(sums, points, live_count, constants[0], linear(first_vectors), linear(second_vectors))
    return out.reshape(PAIRS, 1, B * B)


def solution(mesh):
    return jax.shard_map(
        body,
        mesh=mesh,
        in_specs=(
            P("row", "ba", None),
            P("row", None, "ba", None),
            P(),
            P("row"),
            P("row", None),
            P(),
            P("row", None),
            P("row", None, None),
            P("row", None, None),
        ),
        out_specs=P("row", "ba", None),
        check_vma=False,
    )
```

```python
import functools
import math

import jax
import jax.numpy as jnp
from jax import lax
from jax.experimental import pallas as pl
from jax.experimental.pallas import tpu as pltpu
from jax.sharding import PartitionSpec as P

B = 192
G = 32
Z, X = 8, 4
Q = 2 * X
R = Z * Q
LANES = 128
TILES = B * B // LANES
SHARE = TILES // Q
J = 3
TT = SHARE // J
BLK = 2 * TT
HALF = Q // 2
PAIRS = 8
KO = 2 * PAIRS
MESH = pl.DeviceIdType.MESH
F32 = jnp.float32
BF16 = jnp.bfloat16


def split(value):
    high = value.astype(BF16)
    return high, (value - high.astype(F32)).astype(BF16)


def dot(a, b):
    return lax.dot_general(a, b, (((1,), (0,)), ((), ())), preferred_element_type=F32)


def dot3(ah, al, bh, bl):
    return dot(ah, bh) + dot(al, bh) + dot(ah, bl)


def kernel(
    modes_ref, owner_ref, live_ref, triplets_ref, center_ref, points_ref,
    const_ref, first_ref, second_ref, out_ref,
    modes_v, owner_s, live_s, triplets_s, center_s, points_v,
    const_v, first_v, second_v, tile, got1, got2, rot, lhs, term, part1, part2, final,
    gathered, phase_out, phase_in, square, first_t, second_m,
    small_sem, const_sem, second_sem, first_sem,
    s1, r1, s2, r2, sy1, ry1, sy2, ry2, sc, rc, sz, rz, sp, rp,
):
    row = lax.axis_index("row")
    y = lax.axis_index("ba")
    z = row // Q
    q = row % Q
    x = q // 2
    core = q % 2
    ya = y + 1 - 2 * (y % 2)
    yb = 3 - y
    y2 = (y + 2) % 4

    def qpeer(i):
        return ((x + i // 2) % X) * 2 + (core + i % 2) % 2

    def zpeer(i):
        return (z + i) % Z

    barrier = pltpu.get_barrier_semaphore()
    for i in range(1, Z):
        pl.semaphore_signal(barrier, inc=1, device_id=(zpeer(i) * Q + q, y), device_id_type=MESH)
    for i in range(1, Q):
        pl.semaphore_signal(barrier, inc=1, device_id=(z * Q + qpeer(i), y), device_id_type=MESH)
    for other in (ya, yb):
        pl.semaphore_signal(barrier, inc=1, device_id=(row, other), device_id_type=MESH)

    def local(src, dst, sem):
        copy = pltpu.make_async_copy(src, dst, sem)
        copy.start()
        return copy

    small = [
        local(src, dst, small_sem.at[n])
        for n, (src, dst) in enumerate((
            (modes_ref, modes_v), (owner_ref, owner_s), (live_ref, live_s),
            (triplets_ref, triplets_s), (center_ref, center_s), (points_ref, points_v),
        ))
    ]
    first_copies = [
        local(
            first_ref.at[:, p, pl.ds(j * BLK, BLK), :],
            first_v.at[j, :, pl.ds(p * BLK, BLK), :],
            first_sem.at[j, p],
        )
        for j in range(J) for p in range(Q)
    ]
    second_copy = local(second_ref, second_v, second_sem)
    const_copies = {
        (j, p): local(
            const_ref.at[:, pl.ds((p * SHARE + j * TT) * LANES, TT * LANES)],
            const_v.at[j, p],
            const_sem.at[j, p],
        )
        for j in range(J) for p in range(Q)
    }

    tile[...] = jnp.zeros_like(tile)
    for copy in small:
        copy.wait()
    mine = jnp.where(owner_s[0] == row, 1.0, 0.0)
    for n in range(4):
        for s in range(2):
            tile[2 * n + s : 2 * n + s + 1, 0:48] = modes_v[s, n : n + 1, :] * mine
    tile[0:8] = tile[0:8] + pltpu.roll(tile[0:8], 48, 1)
    second_cell = [triplets_s[0, 3 + axis] for axis in range(3)]
    numbers = [triplets_s[0, axis] - second_cell[axis] for axis in range(3)]
    shift = sum(second_cell[axis] * center_s[axis] for axis in range(3)) % G
    lane8 = lax.broadcasted_iota(jnp.int32, (8, LANES), 1)
    line8 = lax.broadcasted_iota(jnp.int32, (8, LANES), 0)
    geometry = jnp.zeros((8, LANES), jnp.int32)
    for n, number in enumerate(numbers + [shift]):
        geometry = jnp.where(line8 == n, number, geometry)
    tile[8:16] = jnp.where(lane8 % R == row, geometry.astype(F32), 0.0)
    tile[16:19, 0:PAIRS] = points_v[...].astype(F32)
    points = tile[16:24]
    low_group = jnp.where(lane8 < 4, points, 0.0)
    high_group = points - low_group
    tile[16:24] = (
        low_group + pltpu.roll(low_group, 4, 1) + pltpu.roll(high_group, 4, 1) + pltpu.roll(high_group, 8, 1)
    )
    pl.semaphore_wait(barrier, Z - 1 + Q - 1 + 2)

    def remote(src, dst, send, recv, device):
        return pltpu.make_async_remote_copy(
            src_ref=src, dst_ref=dst, send_sem=send, recv_sem=recv,
            device_id=device, device_id_type=MESH,
        )

    copies1 = []
    for i in range(1, Z):
        copy = remote(tile.at[0:16], got1.at[i], s1.at[i], r1.at[i], (zpeer(i) * Q + q, y))
        copy.start()
        copies1.append(copy)

    def paired(ref, k, start, stride):
        tiles = [ref[k, pl.ds(start + stride // 3 * i, B // 2, stride=stride), :] for i in range(3)]
        return both_parities(tiles)

    def both_parities(tiles):
        even = jnp.concatenate(tiles[0:2], axis=1)
        odd = pltpu.roll(jnp.concatenate(tiles[1:3], axis=1), 192, 1)
        return even, odd

    def prepare_second(k, carry):
        for o in range(2):
            even, odd = paired(second_v, k, o, 6)
            for i in range(2):
                lanes = slice(i * LANES, (i + 1) * LANES)
                square[i, pl.ds(0, B // 2, stride=2), :] = even[:, lanes]
                square[i, pl.ds(1, B // 2, stride=2), :] = odd[:, lanes]
            high, low = split(jnp.concatenate([square[0, 0:B, :], square[1, 0:B, :]], axis=1))
            zero = jnp.zeros((256 - B, 256), BF16)
            second_m[k, o, 0] = jnp.concatenate([high, zero], axis=0)
            second_m[k, o, 1] = jnp.concatenate([low, zero], axis=0)
        return carry

    def prepare_first(k, carry):
        for o in range(2):
            lines = []
            for j in range(J):
                lines += both_parities(
                    [first_v[j, k, pl.ds(2 * i + o, B // 2 // J, stride=6), :] for i in range(3)]
                )
            zero = jnp.zeros((256 - B, 256), F32)
            turned = jnp.transpose(jnp.concatenate(lines + [zero], axis=0))
            for i in range(2):
                lanes = slice(i * LANES, (i + 1) * LANES)
                square[i] = turned[:, lanes]
                for parity in range(2):
                    high, low = split(square[i, pl.ds(parity, B // 2, stride=2), :])
                    rows = slice(parity * (B // 2), (parity + 1) * (B // 2))
                    first_t[k, o, 0, rows, lanes] = high
                    first_t[k, o, 1, rows, lanes] = low
        return carry

    for copy in first_copies:
        copy.wait()
    lax.fori_loop(0, PAIRS, prepare_first, 0)
    for copy in copies1:
        copy.wait_recv()
    total = tile[0:16]
    for i in range(1, Z):
        total = total + got1[i]
    got2[q, 0:16] = total
    got2[q, 16:24] = tile[16:24]
    copies2 = []
    for i in range(1, Q):
        copy = remote(got2.at[q], got2.at[q], s2.at[i], r2.at[i], (z * Q + qpeer(i), y))
        copy.start()
        copies2.append(copy)
    second_copy.wait()
    lax.fori_loop(0, PAIRS, prepare_second, 0)

    for copy in copies2:
        copy.wait_recv()
    total = got2[0, 0:16]
    points = got2[0, 16:24]
    for i in range(1, Q):
        total = total + got2[i, 0:16]
        points = points + pltpu.roll(got2[i, 16:24], KO * i, 1)
    points = jnp.where(line8 == 3, -1.0, points)
    turns = lax.dot_general(
        points, total[8:16], (((0,), (0,)), ((), ())), preferred_element_type=F32
    )
    lane = lax.broadcasted_iota(jnp.int32, (Q * KO, LANES), 1)
    line = lax.broadcasted_iota(jnp.int32, (Q * KO, LANES), 0)
    turns = turns + jnp.where(lane >= R, 8.0, 0.0) - jnp.where(line % 8 >= 4, 8.0, 0.0)
    turns = turns - G * jnp.floor(turns * (1.0 / G))
    high, low = split(jnp.cos(turns * (2.0 * math.pi / G)))
    rot[:, 0:128] = high
    rot[:, 128:256] = low
    eigen = total[0:8] * jnp.where(live_s[0] > 0, 1.0, 0.0)
    high, low = split(eigen)
    lhs[...] = jnp.concatenate(
        [high.astype(F32), jnp.where(lane8 < 48, low.astype(F32), 0.0)], axis=0
    ).astype(BF16)

    def contract(j):
        def step(p, carry):
            pltpu.make_async_copy(const_ref.at[:, pl.ds(0, TT * LANES)], const_v.at[j, p], const_sem.at[j, p]).wait()
            high, low = split(const_v[j, p])
            both = dot(lhs[:, 0:96], jnp.concatenate([high, low], axis=0))
            both = both[0:8] + both[8:16]
            for t in range(TT):
                term[j, p, pl.ds(t, 8, stride=TT), :] = both[:, t * LANES : (t + 1) * LANES]
            return carry

        lax.fori_loop(0, Q, step, 0)

    waits = []

    def go(copy):
        copy.start()
        waits.append(copy)
        return copy

    def band(j, h, n):
        return term.at[j, pl.ds(HALF * h, HALF), pl.ds(pl.multiple_of(n * BLK, 8), BLK), :]

    y1, yy2, c2a, ring, p2a = {}, {}, {}, {}, {}

    def y1_start(j):
        for h, other in enumerate((ya, yb)):
            for slot, n in enumerate((other, y2)):
                y1[j, h, slot] = go(remote(
                    band(j, h, n), part1.at[j, h, slot], sy1.at[j, h, slot], ry1.at[j, h, slot], (row, other)
                ))

    def y2_start(j):
        for h, other in enumerate((yb, ya)):
            y1[j, h, 1].wait_recv()
            mine = band(j, h, other)
            mine[...] = mine[...] + part1[j, h, 1]
            yy2[j, h] = go(remote(mine, part2.at[j, h], sy2.at[j, h], ry2.at[j, h], (row, other)))

    def slot_rows(r, count=1):
        return pl.ds(pl.multiple_of(r * BLK, 8), count * BLK)

    def c2a_start(j):
        for h in range(2):
            y1[j, h, 0].wait_recv()
            yy2[j, h].wait_recv()
            final[j, HALF * h : HALF * (h + 1)] = band(j, h, y)[...] + part1[j, h, 0] + part2[j, h]
        gathered[j, slot_rows(row), :] = final[j, q]
        for i in range(1, Q):
            c2a[j, i] = go(remote(
                final.at[j, qpeer(i)], gathered.at[j, slot_rows(row), :], sc.at[j, i], rc.at[j, i],
                (z * Q + qpeer(i), y),
            ))

    def ring_start(j, i):
        for h in range(2):
            if i == 1 and h == 0:
                for n in range(1, Q):
                    c2a[j, n].wait_recv()
            elif i > 1:
                for side in range(2):
                    ring[j, i - 1, side, h].wait_recv()
            for side, sign in enumerate((1, -1)):
                if i == 4 and side != h:
                    continue
                base = ((z + Z - sign * (i - 1)) % Z) * Q + HALF * h
                block = gathered.at[j, slot_rows(base, HALF), :]
                ring[j, i, side, h] = go(remote(
                    block, block, sz.at[j, i, side, h], rz.at[j, i, side, h],
                    (((z + Z + sign) % Z) * Q + q, y),
                ))

    def phase(j):
        for side in range(2):
            ring[j, 4, side, side].wait_recv()

        def step(u, carry):
            cols = []
            for v in range(2):
                t = 2 * u + v
                cols.append(jnp.concatenate(
                    [gathered[j, pl.ds(s * TT + t, R, stride=BLK), :] for s in range(2)], axis=0
                ))
            high, low = split(jnp.concatenate(cols, axis=1))
            value = dot(rot[...], jnp.concatenate([high, high], axis=0)) + dot(rot[:, 0:128], low)
            for v in range(2):
                for d in range(2 * Q):
                    phase_out[j, d % 2, d // 2, pl.ds(pl.multiple_of((2 * u + v) * 8, 8), 8), :] = value[
                        d * 8 : (d + 1) * 8, v * LANES : (v + 1) * LANES
                    ]
            return carry

        lax.fori_loop(0, TT // 2, step, 0)
        rows = pl.ds(pl.multiple_of(q * TT * 8, 8), TT * 8)
        for g in range(2):
            for i in range(1, Q):
                p2a[j, g, i] = go(remote(
                    phase_out.at[j, g, qpeer(i)], phase_in.at[j, g, rows, :], sp.at[j, g, i], rp.at[j, g, i],
                    (z * Q + qpeer(i), y),
                ))
            phase_in[j, g, rows, :] = phase_out[j, g, q]

    contract(0)
    y1_start(0)
    contract(1)
    y1_start(1)
    y2_start(0)
    contract(2)
    y1_start(2)
    y2_start(1)
    c2a_start(0)
    y2_start(2)
    ring_start(0, 1)
    c2a_start(1)
    ring_start(0, 2)
    c2a_start(2)
    ring_start(0, 3)
    ring_start(1, 1)
    ring_start(0, 4)
    ring_start(1, 2)
    phase(0)
    ring_start(1, 3)
    ring_start(2, 1)
    ring_start(1, 4)
    ring_start(2, 2)
    phase(1)
    ring_start(2, 3)
    ring_start(2, 4)
    phase(2)

    def finish(k, carry):
        g = k // 4
        planes = []
        for o in range(2):
            lines = []
            for j in range(J):
                lines += both_parities([
                    phase_in[j, g, pl.ds(8 * i + 4 * o + k % 4, B // 2 // J, stride=24), :]
                    for i in range(3)
                ])
            planes.append(split(jnp.concatenate(lines, axis=0)))
        (prh, prl), (pih, pil) = planes
        wr = (second_m[k, 0, 0], second_m[k, 0, 1])
        wi = (second_m[k, 1, 0], second_m[k, 1, 1])
        real = dot3(prh, prl, *wr) - dot3(pih, pil, *wi)
        imag = dot3(prh, prl, *wi) + dot3(pih, pil, *wr)
        zero = jnp.zeros((256 - B, 256), F32)
        tr = split(jnp.concatenate([real, zero], axis=0))
        ti = split(jnp.concatenate([imag, zero], axis=0))
        vr = (first_t[k, 0, 0], first_t[k, 0, 1])
        vi = (first_t[k, 1, 0], first_t[k, 1, 1])
        real = dot3(*vr, *tr) - dot3(*vi, *ti)
        imag = dot3(*vr, *ti) + dot3(*vi, *tr)
        value = (real * real + imag * imag) * (1.0 / R)
        even = value[0 : B // 2]
        odd = pltpu.roll(value[B // 2 : B], 64, 1)
        lane = lax.broadcasted_iota(jnp.int32, (B // 2, LANES), 1)
        out_ref[k, pl.ds(0, B // 2, stride=3), :] = even[:, 0:LANES]
        out_ref[k, pl.ds(1, B // 2, stride=3), :] = jnp.where(
            lane < 64, even[:, LANES:], odd[:, 0:LANES]
        )
        out_ref[k, pl.ds(2, B // 2, stride=3), :] = odd[:, LANES:]
        return carry

    for g in range(2):
        for j in range(J):
            for i in range(1, Q):
                p2a[j, g, i].wait_recv()
        lax.fori_loop(4 * g, 4 * g + 4, finish, 0)
    for copy in copies1 + copies2 + waits:
        copy.wait_send()


def linear(vectors):
    tiles = vectors.reshape(PAIRS, 2, TILES, LANES)
    return tiles.transpose(0, 2, 1, 3).reshape(PAIRS, 2 * TILES, LANES)


def body(
    constants,
    current_modes,
    owner_id,
    live_count,
    triplets,
    center_point,
    pair_points,
    first_vectors,
    second_vectors,
):
    anywhere = pl.BlockSpec(memory_space=pltpu.HBM)
    dma = pltpu.SemaphoreType.DMA
    out = pl.pallas_call(
        kernel,
        out_shape=jax.ShapeDtypeStruct((PAIRS, TILES, LANES), F32),
        in_specs=[anywhere] * 9,
        out_specs=pl.BlockSpec(memory_space=pltpu.VMEM),
        scratch_shapes=[
            pltpu.VMEM((2, 4, 48), F32),
            pltpu.SMEM((1,), jnp.int32),
            pltpu.SMEM((1,), jnp.int32),
            pltpu.SMEM((1, 6), jnp.int32),
            pltpu.SMEM((3,), jnp.int32),
            pltpu.VMEM((3, PAIRS), jnp.int32),
            pltpu.VMEM((J, Q, 48, TT * LANES), F32),
            pltpu.VMEM((J, PAIRS, Q * BLK, LANES), F32),
            pltpu.VMEM((PAIRS, 2 * TILES, LANES), F32),
            pltpu.VMEM((24, LANES), F32),
            pltpu.VMEM((Z, 16, LANES), F32),
            pltpu.VMEM((Q, 24, LANES), F32),
            pltpu.VMEM((Q * KO, 256), BF16),
            pltpu.VMEM((16, LANES), BF16),
            pltpu.VMEM((J, Q, 4 * BLK, LANES), F32),
            pltpu.VMEM((J, 2, 2, HALF, BLK, LANES), F32),
            pltpu.VMEM((J, 2, HALF, BLK, LANES), F32),
            pltpu.VMEM((J, Q, BLK, LANES), F32),
            pltpu.VMEM((J, R * BLK, LANES), F32),
            pltpu.VMEM((J, 2, Q, TT * 8, LANES), F32),
            pltpu.VMEM((J, 2, Q * TT * 8, LANES), F32),
            pltpu.VMEM((2, 256, LANES), F32),
            pltpu.VMEM((PAIRS, 2, 2, B, 256), BF16),
            pltpu.VMEM((PAIRS, 2, 2, 256, 256), BF16),
            dma((6,)), dma((J, Q)), dma, dma((J, Q)),
            dma((Z,)), dma((Z,)), dma((Q,)), dma((Q,)),
            dma((J, 2, 2)), dma((J, 2, 2)), dma((J, 2)), dma((J, 2)),
            dma((J, Q)), dma((J, Q)), dma((J, 5, 2, 2)), dma((J, 5, 2, 2)),
            dma((J, 2, Q)), dma((J, 2, Q)),
        ],
        compiler_params=pltpu.CompilerParams(
            collective_id=0, has_side_effects=True, vmem_limit_bytes=60 * 2**20
        ),
    )(
        current_modes[0].transpose(0, 2, 1), owner_id, live_count, triplets, center_point, pair_points.T,
        constants[0], linear(first_vectors).reshape(PAIRS, Q, 2 * SHARE, LANES), linear(second_vectors),
    )
    return out.reshape(PAIRS, 1, B * B)


def solution(mesh):
    return jax.shard_map(
        body,
        mesh=mesh,
        in_specs=(
            P("row", "ba", None),
            P("row", None, "ba", None),
            P(),
            P("row"),
            P("row", None),
            P(),
            P("row", None),
            P("row", None, None),
            P("row", None, None),
        ),
        out_specs=P("row", "ba", None),
        check_vma=False,
    )
```

```python
import functools
import math

import jax
import jax.numpy as jnp
from jax import lax
from jax.experimental import pallas as pl
from jax.experimental.pallas import tpu as pltpu
from jax.sharding import PartitionSpec as P

B = 192
G = 32
Z, X = 8, 4
Q = 2 * X
R = Z * Q
LANES = 128
TILES = B * B // LANES
SHARE = TILES // Q
PIECES = (8, 8, 8, 12)
J = len(PIECES)
ORDER = (
    "C0", "Y0", "C1", "Y1", "C2", "Y2", "A0", "A1", "a0", "C3", "Y3", "A2",
    "11", "12", "21", "b0", "A3", "22", "31", "13", "P0", "41", "32", "23",
    "P1", "42", "33", "P2", "43", "P3",
)
STARTS = tuple(sum(PIECES[:j]) for j in range(J))
HALF = Q // 2
FAST = 1
PAIRS = 8
KO = 2 * PAIRS
MESH = pl.DeviceIdType.MESH
F32 = jnp.float32
BF16 = jnp.bfloat16


def split(value):
    high = value.astype(BF16)
    return high, (value - high.astype(F32)).astype(BF16)


def dot(a, b):
    return lax.dot_general(a, b, (((1,), (0,)), ((), ())), preferred_element_type=F32)


def dot3(ah, al, bh, bl):
    return dot(ah, bh) + dot(al, bh) + dot(ah, bl)


def kernel(
    modes_ref, owner_ref, live_ref, triplets_ref, center_ref, points_ref,
    const_ref, first_ref, second_ref, out_ref,
    modes_v, owner_s, live_s, triplets_s, center_s, points_v,
    const_v, first_v, second_v, tile, got1, got2, rot, lhs, term, part, final,
    gathered, phase_out, phase_in, square, first_t, second_m, out_v,
    out_sem, small_sem, const_sem, second_sem, first_sem,
    s1, r1, s2, r2, sy, ry, sc, rc, sz, rz, sp, rp,
):
    row = lax.axis_index("row")
    y = lax.axis_index("ba")
    z = row // Q
    q = row % Q
    x = q // 2
    core = q % 2

    def qpeer(i):
        return ((x + i // 2) % X) * 2 + (core + i % 2) % 2

    def zpeer(i):
        return (z + i) % Z

    barrier = pltpu.get_barrier_semaphore()
    for i in range(1, Z):
        pl.semaphore_signal(barrier, inc=1, device_id=(zpeer(i) * Q + q, y), device_id_type=MESH)
    for i in range(1, Q):
        pl.semaphore_signal(barrier, inc=1, device_id=(z * Q + qpeer(i), y), device_id_type=MESH)
    for i in range(1, 4):
        pl.semaphore_signal(barrier, inc=1, device_id=(row, (y + i) % 4), device_id_type=MESH)

    def local(src, dst, sem):
        copy = pltpu.make_async_copy(src, dst, sem)
        copy.start()
        return copy

    small = [
        local(src, dst, small_sem.at[n])
        for n, (src, dst) in enumerate((
            (modes_ref, modes_v), (owner_ref, owner_s), (live_ref, live_s),
            (triplets_ref, triplets_s), (center_ref, center_s), (points_ref, points_v),
        ))
    ]
    const_copies = {
        (j, p): local(
            const_ref.at[:, pl.ds((p * SHARE + STARTS[j]) * LANES, PIECES[j] * LANES)],
            const_v.at[p, :, pl.ds(STARTS[j] * LANES, PIECES[j] * LANES)],
            const_sem.at[j, p],
        )
        for j in range(J) for p in range(Q)
    }
    first_copy = local(first_ref, first_v, first_sem)
    second_copy = local(second_ref, second_v, second_sem)

    tile[...] = jnp.zeros_like(tile)
    for copy in small:
        copy.wait()
    mine = jnp.where(owner_s[0] == row, 1.0, 0.0)
    for n in range(4):
        for s in range(2):
            tile[2 * n + s : 2 * n + s + 1, 0:48] = modes_v[s, n : n + 1, :] * mine
    tile[0:8] = tile[0:8] + pltpu.roll(tile[0:8], 48, 1)
    second_cell = [triplets_s[0, 3 + axis] for axis in range(3)]
    numbers = [triplets_s[0, axis] - second_cell[axis] for axis in range(3)]
    shift = sum(second_cell[axis] * center_s[axis] for axis in range(3)) % G
    lane8 = lax.broadcasted_iota(jnp.int32, (8, LANES), 1)
    line8 = lax.broadcasted_iota(jnp.int32, (8, LANES), 0)
    geometry = jnp.zeros((8, LANES), jnp.int32)
    for n, number in enumerate(numbers + [shift]):
        geometry = jnp.where(line8 == n, number, geometry)
    tile[8:16] = jnp.where(lane8 % R == row, geometry.astype(F32), 0.0)
    tile[16:19, 0:PAIRS] = points_v[...].astype(F32)
    points = tile[16:24]
    low_group = jnp.where(lane8 < 4, points, 0.0)
    high_group = points - low_group
    tile[16:24] = (
        low_group + pltpu.roll(low_group, 4, 1) + pltpu.roll(high_group, 4, 1) + pltpu.roll(high_group, 8, 1)
    )
    pl.semaphore_wait(barrier, Z - 1 + Q - 1 + 3)

    def remote(src, dst, send, recv, device):
        return pltpu.make_async_remote_copy(
            src_ref=src, dst_ref=dst, send_sem=send, recv_sem=recv,
            device_id=device, device_id_type=MESH,
        )

    copies1 = []
    for i in range(1, Z):
        copy = remote(tile.at[0:16], got1.at[i], s1.at[i], r1.at[i], (zpeer(i) * Q + q, y))
        copy.start()
        copies1.append(copy)

    def paired(ref, k, start, stride):
        tiles = [ref[k, pl.ds(start + stride // 3 * i, B // 2, stride=stride), :] for i in range(3)]
        return both_parities(tiles)

    def both_parities(tiles):
        even = jnp.concatenate(tiles[0:2], axis=1)
        odd = pltpu.roll(jnp.concatenate(tiles[1:3], axis=1), 192, 1)
        return even, odd

    def prepare_second(k, carry):
        for o in range(2):
            even, odd = paired(second_v, k, o, 6)
            for i in range(2):
                lanes = slice(i * LANES, (i + 1) * LANES)
                square[i, pl.ds(0, B // 2, stride=2), :] = even[:, lanes]
                square[i, pl.ds(1, B // 2, stride=2), :] = odd[:, lanes]
            high, low = split(jnp.concatenate([square[0, 0:B, :], square[1, 0:B, :]], axis=1))
            zero = jnp.zeros((256 - B, 256), BF16)
            second_m[k, o, 0] = jnp.concatenate([high, zero], axis=0)
            second_m[k, o, 1] = jnp.concatenate([low, zero], axis=0)
        return carry

    def prepare_first(k, carry):
        for o in range(2):
            even, odd = paired(first_v, k, o, 6)
            zero = jnp.zeros((256 - B, 256), F32)
            turned = jnp.transpose(jnp.concatenate([even, odd, zero], axis=0))
            for i in range(2):
                lanes = slice(i * LANES, (i + 1) * LANES)
                square[i] = turned[:, lanes]
                for parity in range(2):
                    high, low = split(square[i, pl.ds(parity, B // 2, stride=2), :])
                    rows = slice(parity * (B // 2), (parity + 1) * (B // 2))
                    first_t[k, o, 0, rows, lanes] = high
                    first_t[k, o, 1, rows, lanes] = low
        return carry

    for copy in copies1:
        copy.wait_recv()
    total = tile[0:16]
    for i in range(1, Z):
        total = total + got1[i]
    got2[q, 0:16] = total
    got2[q, 16:24] = tile[16:24]
    copies2 = []
    for i in range(1, Q):
        copy = remote(got2.at[q], got2.at[q], s2.at[i], r2.at[i], (z * Q + qpeer(i), y))
        copy.start()
        copies2.append(copy)

    for copy in copies2:
        copy.wait_recv()
    total = got2[0, 0:16]
    points = got2[0, 16:24]
    for i in range(1, Q):
        total = total + got2[i, 0:16]
        points = points + pltpu.roll(got2[i, 16:24], KO * i, 1)
    eigen = total[0:8] * jnp.where(live_s[0] > 0, 1.0, 0.0)
    high, low = split(eigen)
    lhs[...] = jnp.concatenate(
        [high.astype(F32), jnp.where(lane8 < 48, low.astype(F32), 0.0)], axis=0
    ).astype(BF16)

    def rotation():
        turns = lax.dot_general(
            jnp.where(line8 == 3, -1.0, points), total[8:16], (((0,), (0,)), ((), ())),
            preferred_element_type=F32,
        )
        lane = lax.broadcasted_iota(jnp.int32, (Q * KO, LANES), 1)
        line = lax.broadcasted_iota(jnp.int32, (Q * KO, LANES), 0)
        turns = turns + jnp.where(lane >= R, 8.0, 0.0) - jnp.where(line % 8 >= 4, 8.0, 0.0)
        turns = turns - G * jnp.floor(turns * (1.0 / G))
        high, low = split(jnp.cos(turns * (2.0 * math.pi / G)))
        rot[:, 0:128] = high
        rot[:, 128:256] = low

    def contract(j):
        tiles = PIECES[j]
        lanes = slice(STARTS[j] * LANES, (STARTS[j] + tiles) * LANES)

        def step(p, carry):
            pltpu.make_async_copy(
                const_ref.at[:, pl.ds(0, tiles * LANES)], const_v.at[p, :, lanes], const_sem.at[j, p]
            ).wait()
            high, low = split(const_v[p, :, lanes])
            both = dot(lhs[:, 0:96], jnp.concatenate([high, low], axis=0))
            both = both[0:8] + both[8:16]
            for t in range(tiles):
                term[p, pl.ds(8 * STARTS[j] + t, 8, stride=tiles), :] = both[:, t * LANES : (t + 1) * LANES]
            return carry

        lax.fori_loop(0, Q, step, 0)

    waits = []

    def go(copy):
        copy.start()
        waits.append(copy)
        return copy

    def rows(j):
        return pl.ds(2 * STARTS[j], 2 * PIECES[j])

    def band(j, n):
        start = pl.multiple_of(8 * STARTS[j] + n * (2 * PIECES[j]), 8)
        return term.at[:, pl.ds(start, 2 * PIECES[j]), :]

    yx, c2a, ring, p2a = {}, {}, {}, {}

    def y_start(j):
        for i in range(1, 4):
            other = (y + i) % 4
            yx[j, i] = go(remote(
                band(j, other), part.at[i, :, rows(j), :], sy.at[j, i], ry.at[j, i], (row, other)
            ))

    def slot_rows(j, r, count=1):
        block = 2 * PIECES[j]
        return pl.ds(pl.multiple_of(R * 2 * STARTS[j] + r * block, 8), count * block)

    def c2a_start(j):
        for i in range(1, 4):
            yx[j, i].wait_recv()
        final[:, rows(j), :] = (
            band(j, y)[...] + part[1, :, rows(j), :] + part[2, :, rows(j), :] + part[3, :, rows(j), :]
        )
        for i in range(1, Q):
            c2a[j, i] = go(remote(
                final.at[qpeer(i), rows(j), :], gathered.at[slot_rows(j, row), :],
                sc.at[j, i], rc.at[j, i], (z * Q + qpeer(i), y),
            ))
        gathered[slot_rows(j, row), :] = final[q, rows(j), :]

    def ring_start(j, i):
        if i == 1:
            for n in range(1, Q):
                c2a[j, n].wait_recv()
        else:
            for side in range(2):
                ring[j, i - 1, side].wait_recv()
        for side, sign in enumerate((1, -1)):
            base = ((z + Z - sign * (i - 1)) % Z) * Q
            block = gathered.at[
                slot_rows(j, base, Q) if i < 4 else slot_rows(j, base + HALF * side, HALF), :
            ]
            ring[j, i, side] = go(remote(
                block, block, sz.at[j, i, side], rz.at[j, i, side], (((z + Z + sign) % Z) * Q + q, y)
            ))

    def ring_send(j, n, side, origin, hops, half=None):
        sign = 1 - 2 * side
        base = ((z + Z - sign * origin) % Z) * Q
        block = gathered.at[
            slot_rows(j, base, Q) if half is None else slot_rows(j, base + HALF * half, HALF), :
        ]
        ring[j, n, side] = go(remote(
            block, block, sz.at[j, n, side], rz.at[j, n, side], (((z + Z + sign * hops) % Z) * Q + q, y)
        ))

    def near_start(j):
        for n in range(1, Q):
            c2a[j, n].wait_recv()
        for hops in (2, 1):
            for side in range(2):
                ring_send(j, hops, side, 0, hops)

    def far_start(j):
        for side in range(2):
            ring[j, 2, side].wait_recv()
        for side in range(2):
            ring_send(j, 4, side, 2, 2, side)
        for side in range(2):
            ring_send(j, 3, side, 2, 1)

    def phase(j):
        tiles = PIECES[j]
        for n in (1, 3, 4) if j < FAST else (4,):
            for side in range(2):
                ring[j, n, side].wait_recv()

        def step(u, carry):
            cols = []
            for v in range(2):
                start = R * 2 * STARTS[j] + 2 * u + v
                cols.append(jnp.concatenate(
                    [gathered[pl.ds(start + s * tiles, R, stride=2 * tiles), :] for s in range(2)], axis=0
                ))
            high, low = split(jnp.concatenate(cols, axis=1))
            value = dot(rot[...], jnp.concatenate([high, high], axis=0)) + dot(rot[:, 0:128], low)
            for v in range(2):
                for d in range(2 * Q):
                    where = pl.ds(pl.multiple_of((STARTS[j] + 2 * u + v) * 8, 8), 8)
                    phase_out[d % 2, d // 2, where, :] = value[
                        d * 8 : (d + 1) * 8, v * LANES : (v + 1) * LANES
                    ]
            return carry

        lax.fori_loop(0, tiles // 2, step, 0)
        mine = pl.ds(STARTS[j] * 8, tiles * 8)
        there = pl.ds(pl.multiple_of((q * SHARE + STARTS[j]) * 8, 8), tiles * 8)
        for g in range(2) if j == J - 1 else (slice(None),):
            n = g if j == J - 1 else 0
            for i in range(1, Q):
                p2a[j, n, i] = go(remote(
                    phase_out.at[g, qpeer(i), mine, :], phase_in.at[g, there, :],
                    sp.at[j, n, i], rp.at[j, n, i], (z * Q + qpeer(i), y),
                ))
        for g in range(2):
            phase_in[g, there, :] = phase_out[g, q, mine, :]

    steps = {
        "C": contract, "Y": y_start, "A": c2a_start, "P": phase, "a": near_start, "b": far_start,
        **{str(i): functools.partial(ring_start, i=i) for i in range(1, 5)},
    }
    for name in ORDER:
        steps[name[0]](int(name[1]))
        if name in ("a0", "10"):
            rotation()
    first_copy.wait()
    lax.fori_loop(0, PAIRS, prepare_first, 0)
    second_copy.wait()
    lax.fori_loop(0, PAIRS, prepare_second, 0)
    late = 2 * (Q - 1)
    for copy in copies1 + copies2 + waits[:-late]:
        copy.wait_send()

    def finish(k, carry):
        g = k // 4
        planes = []
        for o in range(2):
            lines = both_parities(
                [phase_in[g, pl.ds(8 * i + 4 * o + k % 4, B // 2, stride=24), :] for i in range(3)]
            )
            planes.append(split(jnp.concatenate(lines, axis=0)))
        (prh, prl), (pih, pil) = planes
        wr = (second_m[k, 0, 0], second_m[k, 0, 1])
        wi = (second_m[k, 1, 0], second_m[k, 1, 1])
        real = dot3(prh, prl, *wr) - dot3(pih, pil, *wi)
        imag = dot3(prh, prl, *wi) + dot3(pih, pil, *wr)
        zero = jnp.zeros((256 - B, 256), F32)
        tr = split(jnp.concatenate([real, zero], axis=0))
        ti = split(jnp.concatenate([imag, zero], axis=0))
        vr = (first_t[k, 0, 0], first_t[k, 0, 1])
        vi = (first_t[k, 1, 0], first_t[k, 1, 1])
        real = dot3(*vr, *tr) - dot3(*vi, *ti)
        imag = dot3(*vr, *ti) + dot3(*vi, *tr)
        value = (real * real + imag * imag) * (1.0 / R)
        even = value[0 : B // 2]
        odd = pltpu.roll(value[B // 2 : B], 64, 1)
        lane = lax.broadcasted_iota(jnp.int32, (B // 2, LANES), 1)
        out_v[k, pl.ds(0, B // 2, stride=3), :] = even[:, 0:LANES]
        out_v[k, pl.ds(1, B // 2, stride=3), :] = jnp.where(
            lane < 64, even[:, LANES:], odd[:, 0:LANES]
        )
        out_v[k, pl.ds(2, B // 2, stride=3), :] = odd[:, LANES:]
        return carry

    outs = []
    for j in range(J - 1):
        for i in range(1, Q):
            p2a[j, 0, i].wait_recv()
    for g in range(2):
        for i in range(1, Q):
            p2a[J - 1, g, i].wait_recv()
        lax.fori_loop(4 * g, 4 * g + 4, finish, 0)
        outs.append(local(out_v.at[4 * g : 4 * g + 4], out_ref.at[4 * g : 4 * g + 4], out_sem.at[g]))
    for copy in waits[-late:]:
        copy.wait_send()
    for copy in outs:
        copy.wait()


def linear(vectors):
    tiles = vectors.reshape(PAIRS, 2, TILES, LANES)
    return tiles.transpose(0, 2, 1, 3).reshape(PAIRS, 2 * TILES, LANES)


def body(
    constants,
    current_modes,
    owner_id,
    live_count,
    triplets,
    center_point,
    pair_points,
    first_vectors,
    second_vectors,
):
    anywhere = pl.BlockSpec(memory_space=pltpu.HBM)
    dma = pltpu.SemaphoreType.DMA
    out = pl.pallas_call(
        kernel,
        out_shape=jax.ShapeDtypeStruct((PAIRS, TILES, LANES), F32),
        in_specs=[anywhere] * 9,
        out_specs=anywhere,
        scratch_shapes=[
            pltpu.VMEM((2, 4, 48), F32),
            pltpu.SMEM((1,), jnp.int32),
            pltpu.SMEM((1,), jnp.int32),
            pltpu.SMEM((1, 6), jnp.int32),
            pltpu.SMEM((3,), jnp.int32),
            pltpu.VMEM((3, PAIRS), jnp.int32),
            pltpu.VMEM((Q, 48, SHARE * LANES), F32),
            pltpu.VMEM((PAIRS, 2 * TILES, LANES), F32),
            pltpu.VMEM((PAIRS, 2 * TILES, LANES), F32),
            pltpu.VMEM((24, LANES), F32),
            pltpu.VMEM((Z, 16, LANES), F32),
            pltpu.VMEM((Q, 24, LANES), F32),
            pltpu.VMEM((Q * KO, 256), BF16),
            pltpu.VMEM((16, LANES), BF16),
            pltpu.VMEM((Q, 8 * SHARE, LANES), F32),
            pltpu.VMEM((4, Q, 2 * SHARE, LANES), F32),
            pltpu.VMEM((Q, 2 * SHARE, LANES), F32),
            pltpu.VMEM((R * 2 * SHARE, LANES), F32),
            pltpu.VMEM((2, Q, SHARE * 8, LANES), F32),
            pltpu.VMEM((2, Q * SHARE * 8, LANES), F32),
            pltpu.VMEM((2, 256, LANES), F32),
            pltpu.VMEM((PAIRS, 2, 2, B, 256), BF16),
            pltpu.VMEM((PAIRS, 2, 2, 256, 256), BF16),
            pltpu.VMEM((PAIRS, TILES, LANES), F32),
            dma((2,)), dma((6,)), dma((J, Q)), dma, dma,
            dma((Z,)), dma((Z,)), dma((Q,)), dma((Q,)),
            dma((J, 4)), dma((J, 4)),
            dma((J, Q)), dma((J, Q)), dma((J, 5, 2)), dma((J, 5, 2)),
            dma((J, 2, Q)), dma((J, 2, Q)),
        ],
        compiler_params=pltpu.CompilerParams(
            collective_id=0, has_side_effects=True, vmem_limit_bytes=60 * 2**20
        ),
    )(
        current_modes[0].transpose(0, 2, 1), owner_id, live_count, triplets, center_point, pair_points.T,
        constants[0], linear(first_vectors), linear(second_vectors),
    )
    return out.reshape(PAIRS, 1, B * B)


def solution(mesh):
    return jax.shard_map(
        body,
        mesh=mesh,
        in_specs=(
            P("row", "ba", None),
            P("row", None, "ba", None),
            P(),
            P("row"),
            P("row", None),
            P(),
            P("row", None),
            P("row", None, None),
            P("row", None, None),
        ),
        out_specs=P("row", "ba", None),
        check_vma=False,
    )
```

```python
import functools
import math

import jax
import jax.numpy as jnp
from jax import lax
from jax.experimental import pallas as pl
from jax.experimental.pallas import tpu as pltpu
from jax.sharding import PartitionSpec as P

B = 192
G = 32
Z, X = 8, 4
Q = 2 * X
R = Z * Q
LANES = 128
TILES = B * B // LANES
SHARE = TILES // Q
PIECES = (8, 8, 8, 12)
J = len(PIECES)
ORDER = (
    "C0", "Y0", "C1", "Y1", "C2", "Y2", "A0", "A1", "a0", "C3", "Y3", "A2",
    "11", "12", "21", "b0", "A3", "22", "31", "13", "P0", "41", "32", "23",
    "P1", "42", "33", "P2", "43", "P3",
)
STARTS = tuple(sum(PIECES[:j]) for j in range(J))
HALF = Q // 2
FAST = 1
PAIRS = 8
KO = 2 * PAIRS
GROUPS = 4
EACH = PAIRS // GROUPS
SPAN = 2 * EACH
MESH = pl.DeviceIdType.MESH
F32 = jnp.float32
BF16 = jnp.bfloat16


def split(value):
    high = value.astype(BF16)
    return high, (value - high.astype(F32)).astype(BF16)


def dot(a, b):
    return lax.dot_general(a, b, (((1,), (0,)), ((), ())), preferred_element_type=F32)


def dot3(ah, al, bh, bl):
    return dot(ah, bh) + dot(al, bh) + dot(ah, bl)


def kernel(
    modes_ref, owner_ref, live_ref, triplets_ref, center_ref, points_ref,
    const_ref, first_ref, second_ref, out_ref,
    modes_v, owner_s, live_s, triplets_s, center_s, points_v,
    const_v, first_v, second_v, tile, got1, got2, rot, lhs, term, part, final,
    gathered, phase_out, phase_in, square, first_t, second_m, out_v,
    out_sem, small_sem, const_sem, second_sem, first_sem,
    s1, r1, s2, r2, sy, ry, sc, rc, sz, rz, sp, rp,
):
    row = lax.axis_index("row")
    y = lax.axis_index("ba")
    z = row // Q
    q = row % Q
    x = q // 2
    core = q % 2

    def qpeer(i):
        return ((x + i // 2) % X) * 2 + (core + i % 2) % 2

    def zpeer(i):
        return (z + i) % Z

    barrier = pltpu.get_barrier_semaphore()
    for i in range(1, Z):
        pl.semaphore_signal(barrier, inc=1, device_id=(zpeer(i) * Q + q, y), device_id_type=MESH)
    for i in range(1, Q):
        pl.semaphore_signal(barrier, inc=1, device_id=(z * Q + qpeer(i), y), device_id_type=MESH)
    for i in range(1, 4):
        pl.semaphore_signal(barrier, inc=1, device_id=(row, (y + i) % 4), device_id_type=MESH)

    def local(src, dst, sem):
        copy = pltpu.make_async_copy(src, dst, sem)
        copy.start()
        return copy

    small = [
        local(src, dst, small_sem.at[n])
        for n, (src, dst) in enumerate((
            (modes_ref, modes_v), (owner_ref, owner_s), (live_ref, live_s),
            (triplets_ref, triplets_s), (center_ref, center_s), (points_ref, points_v),
        ))
    ]
    const_copies = {
        (j, p): local(
            const_ref.at[:, pl.ds((p * SHARE + STARTS[j]) * LANES, PIECES[j] * LANES)],
            const_v.at[p, :, pl.ds(STARTS[j] * LANES, PIECES[j] * LANES)],
            const_sem.at[j, p],
        )
        for j in range(J) for p in range(Q)
    }
    first_copy = local(first_ref, first_v, first_sem)
    second_copy = local(second_ref, second_v, second_sem)

    tile[...] = jnp.zeros_like(tile)
    for copy in small:
        copy.wait()
    mine = jnp.where(owner_s[0] == row, 1.0, 0.0)
    for n in range(4):
        for s in range(2):
            tile[2 * n + s : 2 * n + s + 1, 0:48] = modes_v[s, n : n + 1, :] * mine
    tile[0:8] = tile[0:8] + pltpu.roll(tile[0:8], 48, 1)
    second_cell = [triplets_s[0, 3 + axis] for axis in range(3)]
    numbers = [triplets_s[0, axis] - second_cell[axis] for axis in range(3)]
    shift = sum(second_cell[axis] * center_s[axis] for axis in range(3)) % G
    lane8 = lax.broadcasted_iota(jnp.int32, (8, LANES), 1)
    line8 = lax.broadcasted_iota(jnp.int32, (8, LANES), 0)
    geometry = jnp.zeros((8, LANES), jnp.int32)
    for n, number in enumerate(numbers + [shift]):
        geometry = jnp.where(line8 == n, number, geometry)
    tile[8:16] = jnp.where(lane8 % R == row, geometry.astype(F32), 0.0)
    tile[16:19, 0:PAIRS] = points_v[...].astype(F32)
    points = tile[16:24]
    spread = jnp.zeros((8, LANES), F32)
    for g in range(GROUPS):
        group = jnp.where(lane8 // EACH == g, points, 0.0)
        for o in range(2):
            by = g * EACH + o * EACH
            spread = spread + (pltpu.roll(group, by, 1) if by else group)
    tile[16:24] = spread
    pl.semaphore_wait(barrier, Z - 1 + Q - 1 + 3)

    def remote(src, dst, send, recv, device):
        return pltpu.make_async_remote_copy(
            src_ref=src, dst_ref=dst, send_sem=send, recv_sem=recv,
            device_id=device, device_id_type=MESH,
        )

    copies1 = []
    for i in range(1, Z):
        copy = remote(tile.at[0:16], got1.at[i], s1.at[i], r1.at[i], (zpeer(i) * Q + q, y))
        copy.start()
        copies1.append(copy)

    def paired(ref, k, start, stride):
        tiles = [ref[k, pl.ds(start + stride // 3 * i, B // 2, stride=stride), :] for i in range(3)]
        return both_parities(tiles)

    def both_parities(tiles):
        even = jnp.concatenate(tiles[0:2], axis=1)
        odd = pltpu.roll(jnp.concatenate(tiles[1:3], axis=1), 192, 1)
        return even, odd

    def prepare_second(k, carry):
        for o in range(2):
            even, odd = paired(second_v, k, o, 6)
            for i in range(2):
                lanes = slice(i * LANES, (i + 1) * LANES)
                square[i, pl.ds(0, B // 2, stride=2), :] = even[:, lanes]
                square[i, pl.ds(1, B // 2, stride=2), :] = odd[:, lanes]
            high, low = split(jnp.concatenate([square[0, 0:B, :], square[1, 0:B, :]], axis=1))
            zero = jnp.zeros((256 - B, 256), BF16)
            second_m[k, o, 0] = jnp.concatenate([high, zero], axis=0)
            second_m[k, o, 1] = jnp.concatenate([low, zero], axis=0)
        return carry

    def prepare_first(k, carry):
        for o in range(2):
            even, odd = paired(first_v, k, o, 6)
            zero = jnp.zeros((256 - B, 256), F32)
            turned = jnp.transpose(jnp.concatenate([even, odd, zero], axis=0))
            for i in range(2):
                lanes = slice(i * LANES, (i + 1) * LANES)
                square[i] = turned[:, lanes]
                for parity in range(2):
                    high, low = split(square[i, pl.ds(parity, B // 2, stride=2), :])
                    rows = slice(parity * (B // 2), (parity + 1) * (B // 2))
                    first_t[k, o, 0, rows, lanes] = high
                    first_t[k, o, 1, rows, lanes] = low
        return carry

    for copy in copies1:
        copy.wait_recv()
    total = tile[0:16]
    for i in range(1, Z):
        total = total + got1[i]
    got2[q, 0:16] = total
    got2[q, 16:24] = tile[16:24]
    copies2 = []
    for i in range(1, Q):
        copy = remote(got2.at[q], got2.at[q], s2.at[i], r2.at[i], (z * Q + qpeer(i), y))
        copy.start()
        copies2.append(copy)

    for copy in copies2:
        copy.wait_recv()
    total = got2[0, 0:16]
    points = got2[0, 16:24]
    for i in range(1, Q):
        total = total + got2[i, 0:16]
        points = points + pltpu.roll(got2[i, 16:24], KO * i, 1)
    eigen = total[0:8] * jnp.where(live_s[0] > 0, 1.0, 0.0)
    high, low = split(eigen)
    lhs[...] = jnp.concatenate(
        [high.astype(F32), jnp.where(lane8 < 48, low.astype(F32), 0.0)], axis=0
    ).astype(BF16)

    def rotation():
        turns = lax.dot_general(
            jnp.where(line8 == 3, -1.0, points), total[8:16], (((0,), (0,)), ((), ())),
            preferred_element_type=F32,
        )
        lane = lax.broadcasted_iota(jnp.int32, (Q * KO, LANES), 1)
        line = lax.broadcasted_iota(jnp.int32, (Q * KO, LANES), 0)
        turns = turns + jnp.where(lane >= R, 8.0, 0.0) - jnp.where(line % SPAN >= EACH, 8.0, 0.0)
        turns = turns - G * jnp.floor(turns * (1.0 / G))
        high, low = split(jnp.cos(turns * (2.0 * math.pi / G)))
        rot[:, 0:128] = high
        rot[:, 128:256] = low

    def contract(j):
        tiles = PIECES[j]
        lanes = slice(STARTS[j] * LANES, (STARTS[j] + tiles) * LANES)

        def step(p, carry):
            pltpu.make_async_copy(
                const_ref.at[:, pl.ds(0, tiles * LANES)], const_v.at[p, :, lanes], const_sem.at[j, p]
            ).wait()
            high, low = split(const_v[p, :, lanes])
            both = dot(lhs[:, 0:96], jnp.concatenate([high, low], axis=0))
            both = both[0:8] + both[8:16]
            for t in range(tiles):
                term[p, pl.ds(8 * STARTS[j] + t, 8, stride=tiles), :] = both[:, t * LANES : (t + 1) * LANES]
            return carry

        lax.fori_loop(0, Q, step, 0)

    waits = []

    def go(copy):
        copy.start()
        waits.append(copy)
        return copy

    def rows(j):
        return pl.ds(2 * STARTS[j], 2 * PIECES[j])

    def band(j, n):
        start = pl.multiple_of(8 * STARTS[j] + n * (2 * PIECES[j]), 8)
        return term.at[:, pl.ds(start, 2 * PIECES[j]), :]

    yx, c2a, ring, p2a = {}, {}, {}, {}

    def y_start(j):
        for i in range(1, 4):
            other = (y + i) % 4
            yx[j, i] = go(remote(
                band(j, other), part.at[i, :, rows(j), :], sy.at[j, i], ry.at[j, i], (row, other)
            ))

    def slot_rows(j, r, count=1):
        block = 2 * PIECES[j]
        return pl.ds(pl.multiple_of(R * 2 * STARTS[j] + r * block, 8), count * block)

    def c2a_start(j):
        for i in range(1, 4):
            yx[j, i].wait_recv()
        final[:, rows(j), :] = (
            band(j, y)[...] + part[1, :, rows(j), :] + part[2, :, rows(j), :] + part[3, :, rows(j), :]
        )
        for i in range(1, Q):
            c2a[j, i] = go(remote(
                final.at[qpeer(i), rows(j), :], gathered.at[slot_rows(j, row), :],
                sc.at[j, i], rc.at[j, i], (z * Q + qpeer(i), y),
            ))
        gathered[slot_rows(j, row), :] = final[q, rows(j), :]

    def ring_start(j, i):
        if i == 1:
            for n in range(1, Q):
                c2a[j, n].wait_recv()
        else:
            for side in range(2):
                ring[j, i - 1, side].wait_recv()
        for side, sign in enumerate((1, -1)):
            base = ((z + Z - sign * (i - 1)) % Z) * Q
            block = gathered.at[
                slot_rows(j, base, Q) if i < 4 else slot_rows(j, base + HALF * side, HALF), :
            ]
            ring[j, i, side] = go(remote(
                block, block, sz.at[j, i, side], rz.at[j, i, side], (((z + Z + sign) % Z) * Q + q, y)
            ))

    def ring_send(j, n, side, origin, hops, half=None):
        sign = 1 - 2 * side
        base = ((z + Z - sign * origin) % Z) * Q
        block = gathered.at[
            slot_rows(j, base, Q) if half is None else slot_rows(j, base + HALF * half, HALF), :
        ]
        ring[j, n, side] = go(remote(
            block, block, sz.at[j, n, side], rz.at[j, n, side], (((z + Z + sign * hops) % Z) * Q + q, y)
        ))

    def near_start(j):
        for n in range(1, Q):
            c2a[j, n].wait_recv()
        for hops in (2, 1):
            for side in range(2):
                ring_send(j, hops, side, 0, hops)

    def far_start(j):
        for side in range(2):
            ring[j, 2, side].wait_recv()
        for side in range(2):
            ring_send(j, 4, side, 2, 2, side)
        for side in range(2):
            ring_send(j, 3, side, 2, 1)

    def phase(j):
        tiles = PIECES[j]
        for n in (1, 3, 4) if j < FAST else (4,):
            for side in range(2):
                ring[j, n, side].wait_recv()

        def step(u, carry):
            cols = []
            for v in range(2):
                start = R * 2 * STARTS[j] + 2 * u + v
                cols.append(jnp.concatenate(
                    [gathered[pl.ds(start + s * tiles, R, stride=2 * tiles), :] for s in range(2)], axis=0
                ))
            high, low = split(jnp.concatenate(cols, axis=1))
            value = dot(rot[...], jnp.concatenate([high, high], axis=0)) + dot(rot[:, 0:128], low)
            where = pl.ds(pl.multiple_of((STARTS[j] + 2 * u) * SPAN, 8), 2 * SPAN)
            for d in range(GROUPS * Q):
                lines = value[d * SPAN : (d + 1) * SPAN]
                phase_out[d % GROUPS, d // GROUPS, where, :] = jnp.concatenate(
                    [lines[:, 0:LANES], lines[:, LANES : 2 * LANES]], axis=0
                )
            return carry

        lax.fori_loop(0, tiles // 2, step, 0)
        mine = pl.ds(STARTS[j] * SPAN, tiles * SPAN)
        there = pl.ds(pl.multiple_of((q * SHARE + STARTS[j]) * SPAN, 8), tiles * SPAN)
        for g in range(GROUPS) if j == J - 1 else (slice(None),):
            n = g if j == J - 1 else 0
            for i in range(1, Q):
                p2a[j, n, i] = go(remote(
                    phase_out.at[g, qpeer(i), mine, :], phase_in.at[g, there, :],
                    sp.at[j, n, i], rp.at[j, n, i], (z * Q + qpeer(i), y),
                ))
        for g in range(GROUPS):
            phase_in[g, there, :] = phase_out[g, q, mine, :]

    steps = {
        "C": contract, "Y": y_start, "A": c2a_start, "P": phase, "a": near_start, "b": far_start,
        **{str(i): functools.partial(ring_start, i=i) for i in range(1, 5)},
    }
    for name in ORDER:
        steps[name[0]](int(name[1]))
        if name in ("a0", "10"):
            rotation()
    first_copy.wait()
    lax.fori_loop(0, PAIRS, prepare_first, 0)
    second_copy.wait()
    lax.fori_loop(0, PAIRS, prepare_second, 0)
    late = GROUPS * (Q - 1)
    for copy in copies1 + copies2 + waits[:-late]:
        copy.wait_send()

    def finish(k, carry):
        g = k // EACH
        planes = []
        for o in range(2):
            lines = both_parities(
                [phase_in[g, pl.ds(SPAN * i + EACH * o + k % EACH, B // 2, stride=3 * SPAN), :] for i in range(3)]
            )
            planes.append(split(jnp.concatenate(lines, axis=0)))
        (prh, prl), (pih, pil) = planes
        wr = (second_m[k, 0, 0], second_m[k, 0, 1])
        wi = (second_m[k, 1, 0], second_m[k, 1, 1])
        real = dot3(prh, prl, *wr) - dot3(pih, pil, *wi)
        imag = dot3(prh, prl, *wi) + dot3(pih, pil, *wr)
        zero = jnp.zeros((256 - B, 256), F32)
        tr = split(jnp.concatenate([real, zero], axis=0))
        ti = split(jnp.concatenate([imag, zero], axis=0))
        vr = (first_t[k, 0, 0], first_t[k, 0, 1])
        vi = (first_t[k, 1, 0], first_t[k, 1, 1])
        real = dot3(*vr, *tr) - dot3(*vi, *ti)
        imag = dot3(*vr, *ti) + dot3(*vi, *tr)
        value = (real * real + imag * imag) * (1.0 / R)
        even = value[0 : B // 2]
        odd = pltpu.roll(value[B // 2 : B], 64, 1)
        lane = lax.broadcasted_iota(jnp.int32, (B // 2, LANES), 1)
        out_v[k, pl.ds(0, B // 2, stride=3), :] = even[:, 0:LANES]
        out_v[k, pl.ds(1, B // 2, stride=3), :] = jnp.where(
            lane < 64, even[:, LANES:], odd[:, 0:LANES]
        )
        out_v[k, pl.ds(2, B // 2, stride=3), :] = odd[:, LANES:]
        return carry

    outs = []
    for j in range(J - 1):
        for i in range(1, Q):
            p2a[j, 0, i].wait_recv()
    for g in range(GROUPS):
        for i in range(1, Q):
            p2a[J - 1, g, i].wait_recv()
        lax.fori_loop(EACH * g, EACH * (g + 1), finish, 0)
        done = pl.ds(EACH * g, EACH)
        outs.append(local(out_v.at[done], out_ref.at[done], out_sem.at[g]))
    for copy in waits[-late:]:
        copy.wait_send()
    for copy in outs:
        copy.wait()


def linear(vectors):
    tiles = vectors.reshape(PAIRS, 2, TILES, LANES)
    return tiles.transpose(0, 2, 1, 3).reshape(PAIRS, 2 * TILES, LANES)


def body(
    constants,
    current_modes,
    owner_id,
    live_count,
    triplets,
    center_point,
    pair_points,
    first_vectors,
    second_vectors,
):
    anywhere = pl.BlockSpec(memory_space=pltpu.HBM)
    dma = pltpu.SemaphoreType.DMA
    out = pl.pallas_call(
        kernel,
        out_shape=jax.ShapeDtypeStruct((PAIRS, TILES, LANES), F32),
        in_specs=[anywhere] * 9,
        out_specs=anywhere,
        scratch_shapes=[
            pltpu.VMEM((2, 4, 48), F32),
            pltpu.SMEM((1,), jnp.int32),
            pltpu.SMEM((1,), jnp.int32),
            pltpu.SMEM((1, 6), jnp.int32),
            pltpu.SMEM((3,), jnp.int32),
            pltpu.VMEM((3, PAIRS), jnp.int32),
            pltpu.VMEM((Q, 48, SHARE * LANES), F32),
            pltpu.VMEM((PAIRS, 2 * TILES, LANES), F32),
            pltpu.VMEM((PAIRS, 2 * TILES, LANES), F32),
            pltpu.VMEM((24, LANES), F32),
            pltpu.VMEM((Z, 16, LANES), F32),
            pltpu.VMEM((Q, 24, LANES), F32),
            pltpu.VMEM((Q * KO, 256), BF16),
            pltpu.VMEM((16, LANES), BF16),
            pltpu.VMEM((Q, 8 * SHARE, LANES), F32),
            pltpu.VMEM((4, Q, 2 * SHARE, LANES), F32),
            pltpu.VMEM((Q, 2 * SHARE, LANES), F32),
            pltpu.VMEM((R * 2 * SHARE, LANES), F32),
            pltpu.VMEM((GROUPS, Q, SHARE * SPAN, LANES), F32),
            pltpu.VMEM((GROUPS, Q * SHARE * SPAN, LANES), F32),
            pltpu.VMEM((2, 256, LANES), F32),
            pltpu.VMEM((PAIRS, 2, 2, B, 256), BF16),
            pltpu.VMEM((PAIRS, 2, 2, 256, 256), BF16),
            pltpu.VMEM((PAIRS, TILES, LANES), F32),
            dma((GROUPS,)), dma((6,)), dma((J, Q)), dma, dma,
            dma((Z,)), dma((Z,)), dma((Q,)), dma((Q,)),
            dma((J, 4)), dma((J, 4)),
            dma((J, Q)), dma((J, Q)), dma((J, 5, 2)), dma((J, 5, 2)),
            dma((J, GROUPS, Q)), dma((J, GROUPS, Q)),
        ],
        compiler_params=pltpu.CompilerParams(
            collective_id=0, has_side_effects=True, vmem_limit_bytes=60 * 2**20
        ),
    )(
        current_modes[0].transpose(0, 2, 1), owner_id, live_count, triplets, center_point, pair_points.T,
        constants[0], linear(first_vectors), linear(second_vectors),
    )
    return out.reshape(PAIRS, 1, B * B)


def solution(mesh):
    return jax.shard_map(
        body,
        mesh=mesh,
        in_specs=(
            P("row", "ba", None),
            P("row", None, "ba", None),
            P(),
            P("row"),
            P("row", None),
            P(),
            P("row", None),
            P("row", None, None),
            P("row", None, None),
        ),
        out_specs=P("row", "ba", None),
        check_vma=False,
    )
```

```python
import functools
import math

import jax
import jax.numpy as jnp
from jax import lax
from jax.experimental import pallas as pl
from jax.experimental.pallas import tpu as pltpu
from jax.sharding import PartitionSpec as P

B = 192
G = 32
Z, X = 8, 4
Q = 2 * X
R = Z * Q
LANES = 128
TILES = B * B // LANES
SHARE = TILES // Q
PIECES = (8, 8, 8, 12)
J = len(PIECES)
ORDER = (
    "C0", "Y0", "C1", "Y1", "C2", "Y2", "A0", "A1", "10", "C3", "Y3", "A2",
    "11", "20", "12", "21", "30", "A3", "22", "31", "40", "13", "P0", "41",
    "32", "23", "P1", "42", "33", "P2", "43", "P3",
)
STARTS = tuple(sum(PIECES[:j]) for j in range(J))
HALF = Q // 2
PAIRS = 8
KO = 2 * PAIRS
GROUPS = 4
EACH = PAIRS // GROUPS
SPAN = 2 * EACH
MESH = pl.DeviceIdType.MESH
F32 = jnp.float32
BF16 = jnp.bfloat16


def split(value):
    high = value.astype(BF16)
    return high, (value - high.astype(F32)).astype(BF16)


def dot(a, b):
    return lax.dot_general(a, b, (((1,), (0,)), ((), ())), preferred_element_type=F32)


def dot3(ah, al, bh, bl):
    return dot(ah, bh) + dot(al, bh) + dot(ah, bl)


def kernel(
    modes_ref, owner_ref, live_ref, triplets_ref, center_ref, points_ref,
    const_ref, first_ref, second_ref, out_ref,
    modes_v, owner_s, live_s, triplets_s, center_s, points_v,
    const_v, first_v, second_v, tile, got1, got2, rot, lhs, term, part, final,
    gathered, phase_out, phase_in, square, first_t, second_m, out_v,
    out_sem, small_sem, const_sem, second_sem, first_sem,
    s1, r1, s2, r2, sy, ry, sc, rc, sz, rz, sp, rp,
):
    row = lax.axis_index("row")
    y = lax.axis_index("ba")
    z = row // Q
    q = row % Q
    x = q // 2
    core = q % 2

    def qpeer(i):
        return ((x + i // 2) % X) * 2 + (core + i % 2) % 2

    def zpeer(i):
        return (z + i) % Z

    barrier = pltpu.get_barrier_semaphore()
    for i in range(1, Z):
        pl.semaphore_signal(barrier, inc=1, device_id=(zpeer(i) * Q + q, y), device_id_type=MESH)
    for i in range(1, Q):
        pl.semaphore_signal(barrier, inc=1, device_id=(z * Q + qpeer(i), y), device_id_type=MESH)
    for i in range(1, 4):
        pl.semaphore_signal(barrier, inc=1, device_id=(row, (y + i) % 4), device_id_type=MESH)

    def local(src, dst, sem):
        copy = pltpu.make_async_copy(src, dst, sem)
        copy.start()
        return copy

    small = [
        local(src, dst, small_sem.at[n])
        for n, (src, dst) in enumerate((
            (modes_ref, modes_v), (owner_ref, owner_s), (live_ref, live_s),
            (triplets_ref, triplets_s), (center_ref, center_s), (points_ref, points_v),
        ))
    ]

    tile[...] = jnp.zeros_like(tile)
    for copy in small:
        copy.wait()
    mine = jnp.where(owner_s[0] == row, 1.0, 0.0)
    for n in range(4):
        for s in range(2):
            tile[2 * n + s : 2 * n + s + 1, 0:48] = modes_v[s, n : n + 1, :] * mine
    tile[0:8] = tile[0:8] + pltpu.roll(tile[0:8], 48, 1)
    second_cell = [triplets_s[0, 3 + axis] for axis in range(3)]
    numbers = [triplets_s[0, axis] - second_cell[axis] for axis in range(3)]
    shift = sum(second_cell[axis] * center_s[axis] for axis in range(3)) % G
    lane8 = lax.broadcasted_iota(jnp.int32, (8, LANES), 1)
    line8 = lax.broadcasted_iota(jnp.int32, (8, LANES), 0)
    geometry = jnp.zeros((8, LANES), jnp.int32)
    for n, number in enumerate(numbers + [shift]):
        geometry = jnp.where(line8 == n, number, geometry)
    tile[8:16] = jnp.where(lane8 % R == row, geometry.astype(F32), 0.0)
    tile[16:19, 0:PAIRS] = points_v[...].astype(F32)
    points = tile[16:24]
    spread = jnp.zeros((8, LANES), F32)
    for g in range(GROUPS):
        group = jnp.where(lane8 // EACH == g, points, 0.0)
        for o in range(2):
            by = g * EACH + o * EACH
            spread = spread + (pltpu.roll(group, by, 1) if by else group)
    tile[16:24] = spread
    pl.semaphore_wait(barrier, Z - 1 + Q - 1 + 3)

    def remote(src, dst, send, recv, device):
        return pltpu.make_async_remote_copy(
            src_ref=src, dst_ref=dst, send_sem=send, recv_sem=recv,
            device_id=device, device_id_type=MESH,
        )

    copies1 = []
    for i in range(1, Z):
        copy = remote(tile.at[0:16], got1.at[i], s1.at[i], r1.at[i], (zpeer(i) * Q + q, y))
        copy.start()
        copies1.append(copy)
    const_copies = {
        (j, p): local(
            const_ref.at[:, pl.ds((p * SHARE + STARTS[j]) * LANES, PIECES[j] * LANES)],
            const_v.at[p, :, pl.ds(STARTS[j] * LANES, PIECES[j] * LANES)],
            const_sem.at[j, p],
        )
        for j in range(J) for p in range(Q)
    }

    def paired(ref, k, start, stride):
        tiles = [ref[k, pl.ds(start + stride // 3 * i, B // 2, stride=stride), :] for i in range(3)]
        return both_parities(tiles)

    def both_parities(tiles):
        even = jnp.concatenate(tiles[0:2], axis=1)
        odd = pltpu.roll(jnp.concatenate(tiles[1:3], axis=1), 192, 1)
        return even, odd

    def prepare_second(k, carry):
        for o in range(2):
            even, odd = paired(second_v, k, o, 6)
            for i in range(2):
                lanes = slice(i * LANES, (i + 1) * LANES)
                square[i, pl.ds(0, B // 2, stride=2), :] = even[:, lanes]
                square[i, pl.ds(1, B // 2, stride=2), :] = odd[:, lanes]
            high, low = split(jnp.concatenate([square[0, 0:B, :], square[1, 0:B, :]], axis=1))
            zero = jnp.zeros((256 - B, 256), BF16)
            second_m[k, o, 0] = jnp.concatenate([high, zero], axis=0)
            second_m[k, o, 1] = jnp.concatenate([low, zero], axis=0)
        return carry

    def prepare_first(k, carry):
        for o in range(2):
            even, odd = paired(first_v, k, o, 6)
            zero = jnp.zeros((256 - B, 256), F32)
            turned = jnp.transpose(jnp.concatenate([even, odd, zero], axis=0))
            for i in range(2):
                lanes = slice(i * LANES, (i + 1) * LANES)
                square[i] = turned[:, lanes]
                for parity in range(2):
                    high, low = split(square[i, pl.ds(parity, B // 2, stride=2), :])
                    rows = slice(parity * (B // 2), (parity + 1) * (B // 2))
                    first_t[k, o, 0, rows, lanes] = high
                    first_t[k, o, 1, rows, lanes] = low
        return carry

    for copy in copies1:
        copy.wait_recv()
    total = tile[0:16]
    for i in range(1, Z):
        total = total + got1[i]
    got2[q, 0:16] = total
    got2[q, 16:24] = tile[16:24]
    copies2 = []
    for i in range(1, Q):
        copy = remote(got2.at[q], got2.at[q], s2.at[i], r2.at[i], (z * Q + qpeer(i), y))
        copy.start()
        copies2.append(copy)

    for copy in copies2:
        copy.wait_recv()
    total = got2[0, 0:16]
    points = got2[0, 16:24]
    for i in range(1, Q):
        total = total + got2[i, 0:16]
        points = points + pltpu.roll(got2[i, 16:24], KO * i, 1)
    eigen = total[0:8] * jnp.where(live_s[0] > 0, 1.0, 0.0)
    high, low = split(eigen)
    lhs[...] = jnp.concatenate(
        [high.astype(F32), jnp.where(lane8 < 48, low.astype(F32), 0.0)], axis=0
    ).astype(BF16)

    def rotation():
        turns = lax.dot_general(
            jnp.where(line8 == 3, -1.0, points), total[8:16], (((0,), (0,)), ((), ())),
            preferred_element_type=F32,
        )
        lane = lax.broadcasted_iota(jnp.int32, (Q * KO, LANES), 1)
        line = lax.broadcasted_iota(jnp.int32, (Q * KO, LANES), 0)
        turns = turns + jnp.where(lane >= R, 8.0, 0.0) - jnp.where(line % SPAN >= EACH, 8.0, 0.0)
        turns = turns - G * jnp.floor(turns * (1.0 / G))
        high, low = split(jnp.cos(turns * (2.0 * math.pi / G)))
        rot[:, 0:128] = high
        rot[:, 128:256] = low

    first_copy = local(first_ref, first_v, first_sem)
    second_copy = local(second_ref, second_v, second_sem)

    def contract(j):
        tiles = PIECES[j]
        lanes = slice(STARTS[j] * LANES, (STARTS[j] + tiles) * LANES)

        def step(p, carry):
            pltpu.make_async_copy(
                const_ref.at[:, pl.ds(0, tiles * LANES)], const_v.at[p, :, lanes], const_sem.at[j, p]
            ).wait()
            high, low = split(const_v[p, :, lanes])
            both = dot(lhs[:, 0:96], jnp.concatenate([high, low], axis=0))
            both = both[0:8] + both[8:16]
            for t in range(tiles):
                term[p, pl.ds(8 * STARTS[j] + t, 8, stride=tiles), :] = both[:, t * LANES : (t + 1) * LANES]
            return carry

        lax.fori_loop(0, Q, step, 0)

    waits = []

    def go(copy):
        copy.start()
        waits.append(copy)
        return copy

    def rows(j):
        return pl.ds(2 * STARTS[j], 2 * PIECES[j])

    def band(j, n):
        start = pl.multiple_of(8 * STARTS[j] + n * (2 * PIECES[j]), 8)
        return term.at[:, pl.ds(start, 2 * PIECES[j]), :]

    yx, c2a, ring, p2a = {}, {}, {}, {}

    def y_start(j):
        for i in range(1, 4):
            other = (y + i) % 4
            yx[j, i] = go(remote(
                band(j, other), part.at[i, :, rows(j), :], sy.at[j, i], ry.at[j, i], (row, other)
            ))

    def slot_rows(j, r, count=1):
        block = 2 * PIECES[j]
        return pl.ds(pl.multiple_of(R * 2 * STARTS[j] + r * block, 8), count * block)

    def c2a_start(j):
        for i in range(1, 4):
            yx[j, i].wait_recv()
        final[:, rows(j), :] = (
            band(j, y)[...] + part[1, :, rows(j), :] + part[2, :, rows(j), :] + part[3, :, rows(j), :]
        )
        for i in range(1, Q):
            c2a[j, i] = go(remote(
                final.at[qpeer(i), rows(j), :], gathered.at[slot_rows(j, row), :],
                sc.at[j, i], rc.at[j, i], (z * Q + qpeer(i), y),
            ))
        gathered[slot_rows(j, row), :] = final[q, rows(j), :]

    def ring_start(j, i):
        if i == 1:
            for n in range(1, Q):
                c2a[j, n].wait_recv()
        else:
            for side in range(2):
                ring[j, i - 1, side].wait_recv()
        for side, sign in enumerate((1, -1)):
            base = ((z + Z - sign * (i - 1)) % Z) * Q
            block = gathered.at[
                slot_rows(j, base, Q) if i < 4 else slot_rows(j, base + HALF * side, HALF), :
            ]
            ring[j, i, side] = go(remote(
                block, block, sz.at[j, i, side], rz.at[j, i, side], (((z + Z + sign) % Z) * Q + q, y)
            ))

    def phase(j):
        tiles = PIECES[j]
        for side in range(2):
            ring[j, 4, side].wait_recv()

        def step(u, carry):
            cols = []
            for v in range(2):
                start = R * 2 * STARTS[j] + 2 * u + v
                cols.append(jnp.concatenate(
                    [gathered[pl.ds(start + s * tiles, R, stride=2 * tiles), :] for s in range(2)], axis=0
                ))
            high, low = split(jnp.concatenate(cols, axis=1))
            value = dot(rot[...], jnp.concatenate([high, high], axis=0)) + dot(rot[:, 0:128], low)
            where = pl.ds(pl.multiple_of((STARTS[j] + 2 * u) * SPAN, 8), 2 * SPAN)
            for d in range(GROUPS * Q):
                lines = value[d * SPAN : (d + 1) * SPAN]
                phase_out[d % GROUPS, d // GROUPS, where, :] = jnp.concatenate(
                    [lines[:, 0:LANES], lines[:, LANES : 2 * LANES]], axis=0
                )
            return carry

        lax.fori_loop(0, tiles // 2, step, 0)
        mine = pl.ds(STARTS[j] * SPAN, tiles * SPAN)
        there = pl.ds(pl.multiple_of((q * SHARE + STARTS[j]) * SPAN, 8), tiles * SPAN)
        for g in range(GROUPS) if j == J - 1 else (slice(None),):
            n = g if j == J - 1 else 0
            for i in range(1, Q):
                p2a[j, n, i] = go(remote(
                    phase_out.at[g, qpeer(i), mine, :], phase_in.at[g, there, :],
                    sp.at[j, n, i], rp.at[j, n, i], (z * Q + qpeer(i), y),
                ))
        for g in range(GROUPS):
            phase_in[g, there, :] = phase_out[g, q, mine, :]

    steps = {
        "C": contract, "Y": y_start, "A": c2a_start, "P": phase,
        **{str(i): functools.partial(ring_start, i=i) for i in range(1, 5)},
    }
    for name in ORDER:
        steps[name[0]](int(name[1]))
        if name == "10":
            rotation()
    first_copy.wait()
    lax.fori_loop(0, PAIRS, prepare_first, 0)
    second_copy.wait()
    lax.fori_loop(0, PAIRS, prepare_second, 0)
    late = GROUPS * (Q - 1)
    for copy in copies1 + copies2 + waits[:-late]:
        copy.wait_send()

    def finish(k, carry):
        g = k // EACH
        planes = []
        for o in range(2):
            lines = both_parities(
                [phase_in[g, pl.ds(SPAN * i + EACH * o + k % EACH, B // 2, stride=3 * SPAN), :] for i in range(3)]
            )
            planes.append(split(jnp.concatenate(lines, axis=0)))
        (prh, prl), (pih, pil) = planes
        wr = (second_m[k, 0, 0], second_m[k, 0, 1])
        wi = (second_m[k, 1, 0], second_m[k, 1, 1])
        real = dot3(prh, prl, *wr) - dot3(pih, pil, *wi)
        imag = dot3(prh, prl, *wi) + dot3(pih, pil, *wr)
        zero = jnp.zeros((256 - B, 256), F32)
        tr = split(jnp.concatenate([real, zero], axis=0))
        ti = split(jnp.concatenate([imag, zero], axis=0))
        vr = (first_t[k, 0, 0], first_t[k, 0, 1])
        vi = (first_t[k, 1, 0], first_t[k, 1, 1])
        real = dot3(*vr, *tr) - dot3(*vi, *ti)
        imag = dot3(*vr, *ti) + dot3(*vi, *tr)
        value = (real * real + imag * imag) * (1.0 / R)
        even = value[0 : B // 2]
        odd = pltpu.roll(value[B // 2 : B], 64, 1)
        lane = lax.broadcasted_iota(jnp.int32, (B // 2, LANES), 1)
        out_v[k, pl.ds(0, B // 2, stride=3), :] = even[:, 0:LANES]
        out_v[k, pl.ds(1, B // 2, stride=3), :] = jnp.where(
            lane < 64, even[:, LANES:], odd[:, 0:LANES]
        )
        out_v[k, pl.ds(2, B // 2, stride=3), :] = odd[:, LANES:]
        return carry

    outs = []
    for j in range(J - 1):
        for i in range(1, Q):
            p2a[j, 0, i].wait_recv()
    for g in range(GROUPS):
        for i in range(1, Q):
            p2a[J - 1, g, i].wait_recv()
        lax.fori_loop(EACH * g, EACH * (g + 1), finish, 0)
        done = pl.ds(EACH * g, EACH)
        outs.append(local(out_v.at[done], out_ref.at[done], out_sem.at[g]))
    for copy in waits[-late:]:
        copy.wait_send()
    for copy in outs:
        copy.wait()


def linear(vectors):
    tiles = vectors.reshape(PAIRS, 2, TILES, LANES)
    return tiles.transpose(0, 2, 1, 3).reshape(PAIRS, 2 * TILES, LANES)


def body(
    constants,
    current_modes,
    owner_id,
    live_count,
    triplets,
    center_point,
    pair_points,
    first_vectors,
    second_vectors,
):
    anywhere = pl.BlockSpec(memory_space=pltpu.HBM)
    dma = pltpu.SemaphoreType.DMA
    out = pl.pallas_call(
        kernel,
        out_shape=jax.ShapeDtypeStruct((PAIRS, TILES, LANES), F32),
        in_specs=[anywhere] * 9,
        out_specs=anywhere,
        scratch_shapes=[
            pltpu.VMEM((2, 4, 48), F32),
            pltpu.SMEM((1,), jnp.int32),
            pltpu.SMEM((1,), jnp.int32),
            pltpu.SMEM((1, 6), jnp.int32),
            pltpu.SMEM((3,), jnp.int32),
            pltpu.VMEM((3, PAIRS), jnp.int32),
            pltpu.VMEM((Q, 48, SHARE * LANES), F32),
            pltpu.VMEM((PAIRS, 2 * TILES, LANES), F32),
            pltpu.VMEM((PAIRS, 2 * TILES, LANES), F32),
            pltpu.VMEM((24, LANES), F32),
            pltpu.VMEM((Z, 16, LANES), F32),
            pltpu.VMEM((Q, 24, LANES), F32),
            pltpu.VMEM((Q * KO, 256), BF16),
            pltpu.VMEM((16, LANES), BF16),
            pltpu.VMEM((Q, 8 * SHARE, LANES), F32),
            pltpu.VMEM((4, Q, 2 * SHARE, LANES), F32),
            pltpu.VMEM((Q, 2 * SHARE, LANES), F32),
            pltpu.VMEM((R * 2 * SHARE, LANES), F32),
            pltpu.VMEM((GROUPS, Q, SHARE * SPAN, LANES), F32),
            pltpu.VMEM((GROUPS, Q * SHARE * SPAN, LANES), F32),
            pltpu.VMEM((2, 256, LANES), F32),
            pltpu.VMEM((PAIRS, 2, 2, B, 256), BF16),
            pltpu.VMEM((PAIRS, 2, 2, 256, 256), BF16),
            pltpu.VMEM((PAIRS, TILES, LANES), F32),
            dma((GROUPS,)), dma((6,)), dma((J, Q)), dma, dma,
            dma((Z,)), dma((Z,)), dma((Q,)), dma((Q,)),
            dma((J, 4)), dma((J, 4)),
            dma((J, Q)), dma((J, Q)), dma((J, 5, 2)), dma((J, 5, 2)),
            dma((J, GROUPS, Q)), dma((J, GROUPS, Q)),
        ],
        compiler_params=pltpu.CompilerParams(
            collective_id=0, has_side_effects=True, vmem_limit_bytes=60 * 2**20
        ),
    )(
        current_modes[0].transpose(0, 2, 1), owner_id, live_count, triplets, center_point, pair_points.T,
        constants[0], linear(first_vectors), linear(second_vectors),
    )
    return out.reshape(PAIRS, 1, B * B)


def solution(mesh):
    return jax.shard_map(
        body,
        mesh=mesh,
        in_specs=(
            P("row", "ba", None),
            P("row", None, "ba", None),
            P(),
            P("row"),
            P("row", None),
            P(),
            P("row", None),
            P("row", None, None),
            P("row", None, None),
        ),
        out_specs=P("row", "ba", None),
        check_vma=False,
    )
```
